256 devices in a mesh: gx: 8 (over y, core), gy: 8 (over z_lo, x), gz: 4 (over z_hi).
Axes of the slice: x: 4, y: 4, z: 8 (z_hi: 4, z_lo: 2; z = z_hi * 2 + z_lo), core: 2. Of those that a mesh axis runs over, the one named last changes fastest.
Arguments:
- latent: float32 [65536, 128], P(('gx', 'gy', 'gz')), may hold values from -6 to 6
- position: float32 [3, 65536], P(None, ('gx', 'gy', 'gz')), may hold values from 0 to 8, as said below
- particle_count: int32 [256], P(('gx', 'gy', 'gz')), may hold values from 64 to 256, as said below
- nbr_count: int32 [65536], P(('gx', 'gy', 'gz')), may hold values from 1 to 16, as said below
- senders: int32 [1048576], P(('gx', 'gy', 'gz')), may hold values from 0 to 639, as said below
- ghost_x: int32 [512, 64], P(('gx', 'gy', 'gz')), may hold values from 0 to 255, as said below
- ghost_y: int32 [512, 64], P(('gx', 'gy', 'gz')), may hold values from 0 to 383, as said below
- ghost_z: int32 [512, 64], P(('gx', 'gy', 'gz')), may hold values from 0 to 511, as said below
- w_send: float32 [128, 128], replicated, may hold values from -0.375 to 0.375
- w_recv: float32 [128, 128], replicated, may hold values from -0.375 to 0.375
- w_geo: float32 [4, 128], replicated, may hold values from -1.5 to 1.5
- w_msg: float32 [128, 128], replicated, may hold values from -0.125 to 0.125
- w_dec: float32 [3, 128], replicated, may hold values from -0.5 to 0.5
- cot_latent: float32 [65536, 128], P(('gx', 'gy', 'gz')), may hold values from -6 to 6
- cot_position: float32 [3, 65536], P(None, ('gx', 'gy', 'gz')), may hold values from -6 to 6
Outputs:
- grad_latent: float32 [65536, 128], P(('gx', 'gy', 'gz'))
- grad_position: float32 [3, 65536], P(None, ('gx', 'gy', 'gz'))
- grad_send: float32 [128, 128], replicated
- grad_recv: float32 [128, 128], replicated
- grad_geo: float32 [4, 128], replicated
- grad_msg: float32 [128, 128], replicated
- grad_dec: float32 [3, 128], replicated
The draws below stay inside these ranges and needn't reach their ends.
Inputs may be any that keep to these rules, and one draw needn't show every extreme that they name: `particle_count`: between 1/4 of the slots and all; some cell is full. `nbr_count`: each particle's first slot is live; every cell has a particle with all 16 slots live. `senders`: a live own row, or a ghost row of the finished table; the last slot of each cell names its last ghost row. `ghost_x`: live own rows; each list's last entry is its cell's last live row. `ghost_y`: live own rows or rows appended along x; each list's last entry is the last such row. `ghost_z`: live own rows or rows appended along x or y; each list's last entry is the last such row. `position`: each particle lies inside its own unit cell.
All inputs are finite; a program needn't handle non-finite values.
Results may differ from the reference program's by a relative error of at most 0.0003.
Values sent between devices are 32-bit elements; how exact they have to be, the bound alone decides.
A program may use at most 192 MiB of HBM per device.

```python
import math
import jax
import jax.numpy as jnp
from jax import lax

LAT = 128
NBR = 16
BLOCK = 128
P_DEV = 256
G_DEV = 64
NDEV = 256
NPART = 65536
N_GX = 8
N_GY = 8
N_GZ = 4


def count_table(key):
    key = jax.random.fold_in(key, 100)
    lowest = P_DEV // 4
    raw = jax.random.randint(key, (NDEV,), 0, 64)
    counts = lowest + (P_DEV - lowest) * raw * raw // 4096
    full = jax.random.randint(jax.random.fold_in(key, 1), (), 0, NDEV)
    return jnp.where(jnp.arange(NDEV) == full, P_DEV, counts).astype(jnp.int32)


def pick_rows(key, counts, extra, width):
    raw = jax.random.randint(key, (NDEV, width), 0, 1 << 20)
    span = (counts + extra)[:, None]
    value = raw % span
    rows = jnp.where(value < counts[:, None], value, P_DEV + value - counts[:, None])
    if extra == 0:
        last = counts - 1
    else:
        last = jnp.full((NDEV,), P_DEV + extra - 1, jnp.int32)
    return rows.at[:, width - 1].set(last).astype(jnp.int32)


def draw_particle_count(key, part):
    counts = count_table(key)
    return counts


def draw_nbr_count(key, part):
    key = jax.random.fold_in(key, 5)
    raw = jax.random.randint(key, (NDEV, P_DEV), 1, NBR + 1)
    return raw.at[:, 0].set(NBR).reshape(NPART).astype(jnp.int32)


def draw_senders(key, part):
    counts = count_table(key)
    key = jax.random.fold_in(key, 4)
    return pick_rows(key, counts, 6 * G_DEV, P_DEV * NBR).reshape(NPART * NBR)


def draw_ghost_x(key, part):
    counts = count_table(key)
    key = jax.random.fold_in(key, 1)
    lists = jnp.stack([pick_rows(jax.random.fold_in(key, 7), counts, 0, G_DEV), pick_rows(jax.random.fold_in(key, 8), counts, 0, G_DEV)], axis=1)
    return lists.reshape(NDEV * 2, G_DEV)


def draw_ghost_y(key, part):
    counts = count_table(key)
    key = jax.random.fold_in(key, 2)
    lists = jnp.stack([pick_rows(jax.random.fold_in(key, 7), counts, 2 * G_DEV, G_DEV), pick_rows(jax.random.fold_in(key, 8), counts, 2 * G_DEV, G_DEV)], axis=1)
    return lists.reshape(NDEV * 2, G_DEV)


def draw_ghost_z(key, part):
    counts = count_table(key)
    key = jax.random.fold_in(key, 3)
    lists = jnp.stack([pick_rows(jax.random.fold_in(key, 7), counts, 4 * G_DEV, G_DEV), pick_rows(jax.random.fold_in(key, 8), counts, 4 * G_DEV, G_DEV)], axis=1)
    return lists.reshape(NDEV * 2, G_DEV)


def draw_position(key, part):
    key = jax.random.fold_in(key, 6)
    inside = jax.random.uniform(key, (3, NDEV, P_DEV), jnp.float32, 0.0, 0.999)
    cells = jnp.arange(NDEV)
    coords = jnp.stack([cells // (N_GY * N_GZ), cells // N_GZ % N_GY, cells % N_GZ]).astype(jnp.float32)
    return (coords[:, :, None] + inside).reshape(3, NPART)


def block_levels(rng, shape, shards, least, high):
    def one(dim, blocks):
        draws = jax.random.uniform(jax.random.fold_in(jax.random.fold_in(rng, 6), dim), (blocks,), jnp.float32, least / len(shards), high / len(shards))
        return jnp.repeat(jnp.exp(draws), shape[dim] // blocks).reshape((-1,) + (1,) * (len(shape) - dim - 1))

    loudness = one(*shards[0])
    for cut in shards[1:]:
        loudness = loudness * one(*cut)
    return loudness


def normal_values(rng, shape, scale, bound, split=(), kind=jnp.bfloat16):
    loudness = block_levels(rng, shape, split, -0.22, 0.18) if split else 1.0
    result = jax.random.normal(rng, shape, jnp.float32) * scale * loudness
    return jnp.minimum(jnp.maximum(result, -bound), bound).astype(kind)


def setup_inputs(seed: int = 0) -> dict:
    splits = jax.random.split(jax.random.key(seed), 16)
    latent = normal_values(splits[0], (NPART, LAT), 1.0, 6.0, ((0, 256),), jnp.float32)
    position = draw_position(jax.random.fold_in(splits[15], 71), 0)
    particle_count = draw_particle_count(jax.random.fold_in(splits[15], 71), 0)
    nbr_count = draw_nbr_count(jax.random.fold_in(splits[15], 71), 0)
    senders = draw_senders(jax.random.fold_in(splits[15], 71), 0)
    ghost_x = draw_ghost_x(jax.random.fold_in(splits[15], 71), 0)
    ghost_y = draw_ghost_y(jax.random.fold_in(splits[15], 71), 0)
    ghost_z = draw_ghost_z(jax.random.fold_in(splits[15], 71), 0)
    w_send = normal_values(splits[8], (LAT, LAT), (2 * LAT) ** -0.5, 0.375, (), jnp.float32)
    w_recv = normal_values(splits[9], (LAT, LAT), (2 * LAT) ** -0.5, 0.375, (), jnp.float32)
    w_geo = normal_values(splits[10], (4, LAT), 16 ** -0.5, 1.5, (), jnp.float32)
    w_msg = normal_values(splits[11], (LAT, LAT), (LAT * NBR) ** -0.5, 0.125, (), jnp.float32)
    w_dec = normal_values(splits[12], (3, LAT), LAT ** -0.5, 0.5, (), jnp.float32)
    cot_latent = normal_values(splits[13], (NPART, LAT), 1.0, 6.0, ((0, 256),), jnp.float32)
    cot_position = normal_values(splits[14], (3, NPART), 1.0, 6.0, ((1, 256),), jnp.float32)
    return {"latent": latent, "position": position, "particle_count": particle_count, "nbr_count": nbr_count, "senders": senders, "ghost_x": ghost_x, "ghost_y": ghost_y, "ghost_z": ghost_z, "w_send": w_send, "w_recv": w_recv, "w_geo": w_geo, "w_msg": w_msg, "w_dec": w_dec, "cot_latent": cot_latent, "cot_position": cot_position}


STRIDE = 0.1
PRECISE = lax.Precision.HIGHEST

def matmul(left, right):
    return jnp.dot(left, right, precision=PRECISE, preferred_element_type=jnp.float32)

def local_step(table_x, table_p, senders, nbr_count, live, w_send, w_recv, w_geo, w_msg, w_dec):
    parts = live.shape[0]
    slots = senders.shape[0] // parts
    blocks = parts // BLOCK
    proj_send = matmul(table_x, w_send)
    own_x = table_x[:parts]
    own_p = table_p[:, :parts]
    proj_recv = matmul(own_x, w_recv)

    def one_block(inputs):
        sender_rows, recv_rows, recv_pos, counts = inputs
        gathered = jnp.take(proj_send, sender_rows, axis=0)
        sender_pos = jnp.take(table_p, sender_rows, axis=1)
        rel = sender_pos - jnp.repeat(recv_pos, slots, axis=1)
        dist = lax.optimization_barrier(jnp.sum(rel * rel, axis=0, keepdims=True))
        geo = jnp.concatenate([rel, dist], axis=0)
        geo_term = lax.dot_general(geo, w_geo, (((0,), (0,)), ((), ())), precision=PRECISE, preferred_element_type=jnp.float32)
        pre = gathered + jnp.repeat(recv_rows, slots, axis=0) + geo_term
        message = matmul(jax.nn.silu(pre), w_msg)
        keep = (jnp.arange(slots)[None, :] < counts[:, None]).astype(message.dtype).reshape(-1, 1)
        return lax.optimization_barrier(jnp.sum((message * keep).reshape(BLOCK, slots, -1), axis=1))
    pos_blocks = jnp.transpose(own_p.reshape(3, blocks, BLOCK), (1, 0, 2))
    agg = lax.map(one_block, (senders.reshape(blocks, BLOCK * slots), proj_recv.reshape(blocks, BLOCK, -1), pos_blocks, nbr_count.reshape(blocks, BLOCK)))
    new_x = own_x + live[:, None] * agg.reshape(parts, -1)
    move = lax.dot_general(w_dec, new_x, (((1,), (1,)), ((), ())), precision=PRECISE, preferred_element_type=jnp.float32)
    new_p = own_p + STRIDE * live[None, :] * move
    return (new_x, new_p)

def build_tables(cells_x, cells_p, lists):
    index = jnp.arange(NDEV)
    coords = (index // (N_GY * N_GZ), index // N_GZ % N_GY, index % N_GZ)
    lengths = (N_GX, N_GY, N_GZ)
    for axis in range(3):
        chosen = lists[axis]
        count = lengths[axis]
        coord = coords[axis]
        send_x = jax.vmap(lambda table, rows: jnp.take(table, rows, axis=0))(cells_x, chosen)
        send_p = jax.vmap(lambda table, rows: jnp.take(table, rows, axis=1))(cells_p, chosen)
        send_p = jnp.transpose(send_p, (0, 2, 1, 3))
        lower = count * (coord == 0).astype(cells_p.dtype)
        upper = -count * (coord == count - 1).astype(cells_p.dtype)
        hot = (jnp.arange(3) == axis).astype(cells_p.dtype)
        offsets = jnp.stack([lower, upper], axis=1)[:, :, None, None] * hot[None, None, :, None]
        send_p = send_p + offsets
        grid_x = send_x.reshape((N_GX, N_GY, N_GZ) + send_x.shape[1:])
        grid_p = send_p.reshape((N_GX, N_GY, N_GZ) + send_p.shape[1:])
        from_prev_x = jnp.roll(grid_x[:, :, :, 1], 1, axis=axis).reshape(NDEV, G_DEV, -1)
        from_next_x = jnp.roll(grid_x[:, :, :, 0], -1, axis=axis).reshape(NDEV, G_DEV, -1)
        from_prev_p = jnp.roll(grid_p[:, :, :, 1], 1, axis=axis).reshape(NDEV, 3, G_DEV)
        from_next_p = jnp.roll(grid_p[:, :, :, 0], -1, axis=axis).reshape(NDEV, 3, G_DEV)
        cells_x = jnp.concatenate([cells_x, from_prev_x, from_next_x], axis=1)
        cells_p = jnp.concatenate([cells_p, from_prev_p, from_next_p], axis=2)
    return (cells_x, cells_p)

def reference(latent, position, particle_count, nbr_count, senders, ghost_x, ghost_y, ghost_z, w_send, w_recv, w_geo, w_msg, w_dec, cot_latent, cot_position):
    lists = (ghost_x.reshape(NDEV, 2, G_DEV), ghost_y.reshape(NDEV, 2, G_DEV), ghost_z.reshape(NDEV, 2, G_DEV))
    live = (jnp.arange(P_DEV)[None, :] < particle_count[:, None]).astype(latent.dtype)
    sender_cells = senders.reshape(NDEV, P_DEV * NBR)
    count_cells = nbr_count.reshape(NDEV, P_DEV)

    def forward(lat, pos, ws, wr, wg, wm, wd):
        cells_x = lat.reshape(NDEV, P_DEV, -1)
        cells_p = jnp.transpose(pos.reshape(3, NDEV, P_DEV), (1, 0, 2))
        step = jax.checkpoint(lambda tx, tp, sn, nc, lv: local_step(tx, tp, sn, nc, lv, ws, wr, wg, wm, wd))
        for turn in range(2):
            table_x, table_p = build_tables(cells_x, cells_p, lists)
            cells_x, cells_p = lax.map(lambda item: step(*item), (table_x, table_p, sender_cells, count_cells, live))
        out_x = cells_x.reshape(NPART, -1)
        out_p = jnp.transpose(cells_p, (1, 0, 2)).reshape(3, NPART)
        return (out_x, out_p)
    outputs, pull = jax.vjp(forward, latent, position, w_send, w_recv, w_geo, w_msg, w_dec)
    grads = pull((cot_latent, cot_position))
    scale = 1.0 / math.sqrt(NPART)
    return (grads[0], grads[1], grads[2] * scale, grads[3] * scale, grads[4] * scale, grads[5] * scale, grads[6] * scale)
```

```python
import functools
import math

import jax
import jax.numpy as jnp
from jax import lax
from jax.experimental import pallas as pl
from jax.experimental.pallas import tpu as pltpu
from jax.sharding import PartitionSpec as P

MESH = pl.DeviceIdType.MESH
AXES = ("gx", "gy", "gz")
F32 = jnp.float32
BF16 = jnp.bfloat16
STRIDE = 0.1
LAT = 128
OWN = 256
NBR = 16
SIDE = 64
GHOST = 2 * SIDE
ROWS = OWN + 3 * GHOST
GRAD_ROWS = 512
MSG = SIDE + 8
UNROLL = 2


def dot(left, right):
    return lax.dot_general(left, right, (((1,), (0,)), ((), ())), preferred_element_type=F32)


def dot_nt(left, right):
    return lax.dot_general(left, right, (((1,), (1,)), ((), ())), preferred_element_type=F32)


def split(value):
    high = value.astype(BF16)
    return high, (value - high.astype(F32)).astype(BF16)


def exact(product, left, right):
    left_high, left_low = split(left)
    right_high, right_low = split(right)
    return product(left_high, right_high) + (product(left_low, right_high) + product(left_high, right_low))


def split_rows(field_x, field_q):
    high, low = split(field_x)
    first = field_q.astype(BF16).astype(F32)
    rest = field_q - first
    second = rest.astype(BF16).astype(F32)
    third = rest - second
    upper = jnp.concatenate([first, second], axis=0).astype(BF16)
    lower = jnp.concatenate([third, jnp.zeros_like(third)], axis=0).astype(BF16)
    return high, low, upper, lower


def join_rows(product):
    value = product[0:LAT] + product[LAT : 2 * LAT]
    base = 2 * LAT
    place = product[base : base + 8] + product[base + 8 : base + 16] + product[base + 16 : base + 24]
    return value, place


def kernel(
    sizes,
    scale,
    latent_ref,
    position_ref,
    senders_ref,
    count_ref,
    ghost_ref,
    particles_ref,
    w_send_ref,
    w_recv_ref,
    w_geo_ref,
    w_msg_ref,
    w_dec_ref,
    cot_latent_ref,
    cot_position_ref,
    out_latent_ref,
    out_position_ref,
    out_send_ref,
    out_recv_ref,
    out_geo_ref,
    out_msg_ref,
    out_dec_ref,
    onehot,
    sel_x,
    sel_y,
    sel_z,
    tab_x,
    tab_q,
    tab_s,
    tab_a,
    gath,
    slope,
    geos,
    summed,
    fresh,
    dpre,
    d_recv,
    d_place,
    cot_x,
    cot_q,
    pad,
    w_t,
    w_geo_k,
    w_geo_s,
    d_geo,
    grads,
    part_x,
    part_y,
    part_z,
    got_x,
    got_y,
    total,
    send_buf,
    recv_buf,
    halo_send,
    halo_recv,
    sum_send,
    sum_recv,
):
    index = tuple(lax.axis_index(axis) for axis in AXES)
    sels = (sel_x, sel_y, sel_z)

    barrier = pltpu.get_barrier_semaphore()
    partners = 0
    for axis in range(3):
        for k in range(1, sizes[axis]):
            peer = lax.rem(index[axis] + k, sizes[axis])
            pl.semaphore_signal(barrier, inc=1, device_id={AXES[axis]: peer}, device_id_type=MESH)
            partners += 1

    lane = lax.broadcasted_iota(jnp.int32, (SIDE, GHOST), 1)
    left = lane < SIDE
    left8 = left[0:8]
    row8 = lax.broadcasted_iota(jnp.int32, (8, GHOST), 0)
    row8_own = lax.broadcasted_iota(jnp.int32, (8, OWN), 0)
    live = (lax.broadcasted_iota(jnp.int32, (1, OWN), 1) < particles_ref[0]).astype(F32)

    pending = []

    def start_halo(phase, axis, field_x, field_q):
        turned = pltpu.roll(field_x, SIDE, 1)
        turned_q = pltpu.roll(field_q, SIDE, 1)
        send_buf[phase, 0, 0:SIDE, :] = jnp.where(left, field_x[0:SIDE], turned[SIDE:])
        send_buf[phase, 0, SIDE:MSG, :] = turned_q
        send_buf[phase, 1, 0:SIDE, :] = jnp.where(left, turned[0:SIDE], field_x[SIDE:])
        send_buf[phase, 1, SIDE:MSG, :] = turned_q
        size = sizes[axis]
        lower = lax.rem(index[axis] + size - 1, size)
        upper = lax.rem(index[axis] + 1, size)
        copies = []
        for side, peer in ((0, lower), (1, upper)):
            copy = pltpu.make_async_remote_copy(
                src_ref=send_buf.at[phase, side],
                dst_ref=recv_buf.at[phase, 1 - side],
                send_sem=halo_send.at[phase, side],
                recv_sem=halo_recv.at[phase, 1 - side],
                device_id={AXES[axis]: peer},
                device_id_type=MESH,
            )
            copy.start()
            copies.append(copy)
        pending.extend(copies)
        return copies

    def end_halo(phase, copies):
        for copy in copies:
            copy.wait_recv()
        before = recv_buf[phase, 0, 0:SIDE, :]
        after = recv_buf[phase, 1, 0:SIDE, :]
        top = jnp.where(left, before, pltpu.roll(after, SIDE, 1))
        bottom = jnp.where(left, pltpu.roll(before, SIDE, 1), after)
        field_q = jnp.where(left8, recv_buf[phase, 0, SIDE:MSG, :], recv_buf[phase, 1, SIDE:MSG, :])
        return jnp.concatenate([top, bottom], axis=0), field_q

    def set_block(step, start, width, field_x, field_q):
        cols = slice(start, start + width)
        tab_x[step, :, cols] = field_x
        tab_q[step, :, cols] = field_q
        high, low, upper, lower = split_rows(field_x, field_q)
        tab_s[0:LAT, cols] = high
        tab_s[LAT : 2 * LAT, cols] = low
        tab_s[256:272, cols] = upper
        tab_s[272:288, cols] = lower

    def project_block(step, start, width):
        cols = slice(start, start + width)
        high, low = split(exact(dot, w_t[0], tab_x[step, :, cols]))
        tab_a[0:LAT, cols] = high
        tab_a[LAT : 2 * LAT, cols] = low
        tab_a[256:288, cols] = tab_s[256:288, cols]

    def select(axis, start, width):
        return dot(tab_s[:, start : start + width], sels[axis][start : start + width, :])

    def send_rows(phase, axis, product):
        field_x, field_q = join_rows(product)
        low = jnp.where(index[axis] == 0, float(sizes[axis]), 0.0)
        high = jnp.where(index[axis] == sizes[axis] - 1, -float(sizes[axis]), 0.0)
        offset = jnp.where(row8 == axis, jnp.where(left8, low, high), 0.0)
        return start_halo(phase, axis, field_x, field_q + offset)

    def gather_block(start, width, extra=None):
        def body(n, carry):
            value, place = join_rows(dot(tab_a[:, start : start + width], onehot[n, start : start + width, :]))
            if extra is None:
                gath[n, 0:LAT, :] += value
                gath[n, LAT:, :] += place
            else:
                gath[n, 0:LAT, :] = value + extra[...]
                gath[n, LAT:, :] = place
            return carry

        lax.fori_loop(0, NBR, body, 0, unroll=UNROLL)

    def forward(step, phase, prologue):
        copies = send_rows(phase, 0, select(0, 0, OWN))
        prologue()
        project_block(step, 0, OWN)
        d_recv[...] = exact(dot, w_t[1], tab_x[step, :, 0:OWN])
        early_y = select(1, 0, OWN)
        early_z = select(2, 0, OWN)
        gather_block(0, OWN, d_recv)
        start = OWN
        set_block(step, start, GHOST, *end_halo(phase, copies))
        copies = send_rows(phase + 1, 1, early_y + select(1, start, GHOST))
        early_z = early_z + select(2, start, GHOST)
        project_block(step, start, GHOST)
        gather_block(start, GHOST)
        start = start + GHOST
        set_block(step, start, GHOST, *end_halo(phase + 1, copies))
        copies = send_rows(phase + 2, 2, early_z + select(2, start, GHOST))
        project_block(step, start, GHOST)
        gather_block(start, GHOST)
        start = start + GHOST
        set_block(step, start, GHOST, *end_halo(phase + 2, copies))
        project_block(step, start, GHOST)
        own_q = tab_q[step, :, 0:OWN]
        counts = count_ref[...]
        summed[step] = jnp.zeros((LAT, OWN), F32)

        def body(n, carry):
            value, place = join_rows(dot(tab_a[:, start : start + GHOST], onehot[n, start : start + GHOST, :]))
            rel = gath[n, LAT:, :] + place - own_q
            dist = jnp.sum(rel * rel, axis=0, keepdims=True)
            geo = jnp.where(row8_own == 3, dist, rel)
            geos[step, n] = geo
            coarse = geo.astype(BF16).astype(F32)
            fine = geo - coarse
            rows = jnp.concatenate([coarse, fine, coarse, jnp.zeros_like(fine)], axis=0).astype(BF16)
            pre = gath[n, 0:LAT, :] + value + dot(w_geo_k[...], rows)
            gate = 0.5 * jnp.tanh(0.5 * pre) + 0.5
            keep = (counts > n).astype(F32)
            gate_keep = gate * keep
            summed[step] += pre * gate_keep
            slope[step, n] = gate_keep * (1.0 + pre * (1.0 - gate))
            return carry

        lax.fori_loop(0, NBR, body, 0, unroll=UNROLL)
        new_x = tab_x[step, :, 0:OWN] + live * exact(dot, w_t[2], summed[step])
        fresh[step] = new_x
        return new_x

    def scatter(start, width):
        def body(n, carry):
            return carry + dot_nt(dpre[n], onehot[n, start : start + width, :])

        product = lax.fori_loop(0, NBR, body, jnp.zeros((272, width), F32), unroll=UNROLL)
        return product[0:LAT] + product[LAT : 2 * LAT], product[256:264] + product[264:272]

    def backward(step, phase, cot_v, cot_p, first, tail):
        move = STRIDE * live * cot_p
        full = cot_v
        for k in range(3):
            full = full + w_t[3, :, k : k + 1] * move[k : k + 1, :]
        d_agg = live * full
        d_sum = exact(dot, w_msg_ref[...], d_agg)
        d_recv[...] = jnp.zeros((LAT, OWN), F32)
        d_place[...] = jnp.zeros((8, OWN), F32)
        d_geo[...] = jnp.zeros((8, LAT), F32)

        def body(n, carry):
            value = d_sum * slope[step, n]
            geo = geos[step, n]
            high, low = split(value)
            dpre[n, 0:LAT, :] = high
            dpre[n, LAT : 2 * LAT, :] = low
            d_recv[...] += value
            main = dot(w_geo_s[...], high)
            side = dot(w_geo_s[...], low)
            back = main[0:8] + main[8:16] + side[0:8]
            d_rel = jnp.where(row8_own < 3, back + 2.0 * geo * back[3:4], 0.0)
            d_place[...] -= d_rel
            coarse = d_rel.astype(BF16).astype(F32)
            dpre[n, 256:272, :] = jnp.concatenate([coarse, d_rel - coarse], axis=0).astype(BF16)
            geo_high = geo.astype(BF16).astype(F32)
            geo_rows = jnp.concatenate([geo_high, geo - geo_high], axis=0).astype(BF16)
            main = dot_nt(geo_rows, high)
            side = dot_nt(geo_rows, low)
            d_geo[...] += main[0:8] + main[8:16] + side[0:8]
            return carry

        lax.fori_loop(0, NBR, body, 0, unroll=UNROLL)

        start = OWN + 2 * GHOST
        d_send, d_q = scatter(start, GHOST)
        copies = start_halo(phase, 2, exact(dot, w_send_ref[...], d_send), d_q)
        d_weight = exact(dot_nt, tab_x[step, :, start : start + GHOST], d_send)
        for start, width in ((OWN + GHOST, GHOST), (OWN, GHOST), (0, OWN)):
            d_send, d_q = scatter(start, width)
            cot_x[:, start : start + width] = exact(dot, w_send_ref[...], d_send)
            cot_q[:, start : start + width] = d_q
            d_weight = d_weight + exact(dot_nt, tab_x[step, :, start : start + width], d_send)
        cot_x[:, 0:OWN] += full + exact(dot, w_recv_ref[...], d_recv[...])
        cot_q[:, 0:OWN] += cot_p + d_place[...]
        pieces = (
            (0, LAT, d_weight),
            (LAT, LAT, exact(dot_nt, tab_x[step, :, 0:OWN], d_recv[...])),
            (2 * LAT, LAT, exact(dot_nt, summed[step], d_agg)),
            (3 * LAT, 8, d_geo[...]),
            (3 * LAT + 8, 8, exact(dot_nt, move, fresh[step])),
        )
        for base, rows, piece in pieces:
            if first:
                grads[base : base + rows, :] = piece
            else:
                grads[base : base + rows, :] += piece
        tail(0)

        def arrived(number, axis, copies):
            field_x, field_q = end_halo(number, copies)
            high, low = split(field_x)
            coarse = field_q.astype(BF16).astype(F32)
            rows = jnp.concatenate([coarse, field_q - coarse], axis=0).astype(BF16)

            def add(start, width):
                sel = sels[axis][start : start + width, :]
                extra = dot_nt(high, sel) + dot_nt(low, sel)
                extra_q = dot_nt(rows, sel)
                cot_x[:, start : start + width] += extra
                cot_q[:, start : start + width] += extra_q[0:8] + extra_q[8:16]

            return add

        add = arrived(phase, 2, copies)
        start = OWN + GHOST
        add(start, GHOST)
        copies = start_halo(phase + 1, 1, cot_x[:, start : start + GHOST], cot_q[:, start : start + GHOST])
        add(OWN, GHOST)
        add(0, OWN)
        add = arrived(phase + 1, 1, copies)
        start = OWN
        add(start, GHOST)
        copies = start_halo(phase + 2, 0, cot_x[:, start : start + GHOST], cot_q[:, start : start + GHOST])
        add(0, OWN)
        tail(1)
        add = arrived(phase + 2, 0, copies)
        add(0, OWN)
        return cot_x[:, 0:OWN], cot_q[:, 0:OWN]

    pad[...] = jnp.zeros((8, OWN), F32)
    pad[0:3, :] = position_ref[...]
    set_block(0, 0, OWN, jnp.transpose(latent_ref[...]), pad[...])
    sel_x[...] = (lax.broadcasted_iota(jnp.int32, (OWN, GHOST), 0) == ghost_ref[0:1, :]).astype(F32).astype(BF16)
    pl.semaphore_wait(barrier, partners)

    def prologue():
        for axis in (1, 2):
            rows = OWN + axis * GHOST
            ids = lax.broadcasted_iota(jnp.int32, (rows, GHOST), 0)
            sels[axis][...] = (ids == ghost_ref[axis : axis + 1, :]).astype(F32).astype(BF16)
        w_t[0] = jnp.transpose(w_send_ref[...])
        w_t[1] = jnp.transpose(w_recv_ref[...])
        w_t[2] = jnp.transpose(w_msg_ref[...])
        w_t[3] = jnp.zeros((LAT, LAT), F32)
        w_t[3, 0:3, :] = w_dec_ref[...]
        w_t[3] = jnp.transpose(w_t[3])
        w_t[4] = jnp.zeros((LAT, LAT), F32)
        w_t[4, 0:4, :] = w_geo_ref[...]
        w_geo = w_t[4, 0:8, :]
        coarse = w_geo.astype(BF16).astype(F32)
        fine = w_geo - coarse
        w_geo_s[...] = jnp.concatenate([coarse, fine], axis=0).astype(BF16)
        w_t[4, 0:8, :] = coarse
        w_t[4, 8:16, :] = coarse
        w_t[4, 16:24, :] = fine
        w_geo_k[...] = jnp.transpose(w_t[4])[:, 0:32].astype(BF16)
        grads[...] = jnp.zeros((GRAD_ROWS, LAT), F32)

        def body(n, carry):
            ids = lax.broadcasted_iota(jnp.int32, (ROWS, OWN), 0)
            onehot[n] = (ids == senders_ref[pl.ds(n, 1), :]).astype(F32).astype(BF16)
            return carry

        lax.fori_loop(0, NBR, body, 0)

    new_x = forward(0, 0, prologue)
    w_dec = jnp.concatenate([w_dec_ref[...], jnp.zeros((5, LAT), F32)], axis=0)
    new_q = tab_q[0, :, 0:OWN] + STRIDE * live * exact(dot, w_dec, new_x)
    set_block(1, 0, OWN, new_x, new_q)
    forward(1, 3, lambda: None)

    pad[0:3, :] = cot_position_ref[...]
    cot_v, cot_p = backward(1, 6, jnp.transpose(cot_latent_ref[...]), pad[...], True, lambda number: None)

    piece_x = GRAD_ROWS // sizes[0]
    piece_y = piece_x // sizes[1]
    bases = (0, sizes[0] - 1, sizes[0] + sizes[1] - 2)
    more = bases[2] + sizes[2] - 1

    def exchange(axis, base, source, target):
        copies = []
        for k in range(1, sizes[axis]):
            peer = lax.rem(index[axis] + k, sizes[axis])
            copy = pltpu.make_async_remote_copy(
                src_ref=source(peer),
                dst_ref=target(k),
                send_sem=sum_send.at[base + k - 1],
                recv_sem=sum_recv.at[base + k - 1],
                device_id={AXES[axis]: peer},
                device_id_type=MESH,
            )
            copy.start()
            copies.append(copy)
        pending.extend(copies)
        return copies

    state = {}

    def tail(number):
        if number == 0:
            state["x"] = exchange(
                0,
                bases[0],
                lambda peer: grads.at[pl.ds(pl.multiple_of(peer * piece_x, 8), piece_x), :],
                lambda k: got_x.at[k - 1],
            )
        else:
            for copy in state["x"]:
                copy.wait_recv()
            value = grads[pl.ds(pl.multiple_of(index[0] * piece_x, 8), piece_x), :]
            for k in range(sizes[0] - 1):
                value = value + got_x[k]
            part_x[...] = value
            state["y"] = exchange(
                1,
                bases[1],
                lambda peer: part_x.at[pl.ds(pl.multiple_of(peer * piece_y, 8), piece_y), :],
                lambda k: got_y.at[k - 1],
            )

    cot_v, cot_p = backward(0, 9, cot_v, cot_p, False, tail)
    for copy in state["y"]:
        copy.wait_recv()
    value = part_x[pl.ds(pl.multiple_of(index[1] * piece_y, 8), piece_y), :]
    for k in range(sizes[1] - 1):
        value = value + got_y[k]
    part_z[index[2]] = value
    copies = exchange(2, bases[2], lambda peer: part_z.at[index[2]], lambda k: part_z.at[index[2]])
    out_latent_ref[...] = jnp.transpose(cot_v)
    out_position_ref[...] = cot_p[0:3]
    for copy in copies:
        copy.wait_recv()
    value = part_z[0]
    for k in range(1, sizes[2]):
        value = value + part_z[k]
    own_y = pl.ds(pl.multiple_of(index[1] * piece_y, 8), piece_y)
    part_y[own_y, :] = value * scale
    copies = exchange(1, more, lambda peer: part_y.at[own_y, :], lambda k: part_y.at[own_y, :])
    for copy in copies:
        copy.wait_recv()
    own_x = pl.ds(pl.multiple_of(index[0] * piece_x, 8), piece_x)
    total[own_x, :] = part_y[...]
    copies = exchange(0, more + sizes[1] - 1, lambda peer: part_y, lambda k: total.at[own_x, :])
    for copy in copies:
        copy.wait_recv()
    out_send_ref[...] = total[0:LAT, :]
    out_recv_ref[...] = total[LAT : 2 * LAT, :]
    out_msg_ref[...] = total[2 * LAT : 3 * LAT, :]
    out_geo_ref[...] = total[3 * LAT : 3 * LAT + 4, :]
    out_dec_ref[...] = total[3 * LAT + 8 : 3 * LAT + 11, :]
    for copy in pending:
        copy.wait_send()


def per_device(sizes, scale, *args):
    (
        latent,
        position,
        particle_count,
        nbr_count,
        senders,
        ghost_x,
        ghost_y,
        ghost_z,
        w_send,
        w_recv,
        w_geo,
        w_msg,
        w_dec,
        cot_latent,
        cot_position,
    ) = args
    slots = jnp.transpose(senders.reshape(OWN, NBR))
    counts = nbr_count.reshape(1, OWN)
    ghosts = jnp.stack([ghost_x.reshape(-1), ghost_y.reshape(-1), ghost_z.reshape(-1)])
    nx, ny, nz = sizes
    piece_x = GRAD_ROWS // nx
    piece_y = piece_x // ny
    sums = 2 * (nx - 1) + 2 * (ny - 1) + (nz - 1)
    vmem = pl.BlockSpec(memory_space=pltpu.VMEM)
    smem = pl.BlockSpec(memory_space=pltpu.SMEM)
    return pl.pallas_call(
        functools.partial(kernel, sizes, scale),
        out_shape=(
            jax.ShapeDtypeStruct((OWN, LAT), F32),
            jax.ShapeDtypeStruct((3, OWN), F32),
            jax.ShapeDtypeStruct((LAT, LAT), F32),
            jax.ShapeDtypeStruct((LAT, LAT), F32),
            jax.ShapeDtypeStruct((4, LAT), F32),
            jax.ShapeDtypeStruct((LAT, LAT), F32),
            jax.ShapeDtypeStruct((3, LAT), F32),
        ),
        in_specs=[vmem] * 5 + [smem] + [vmem] * 7,
        out_specs=(vmem,) * 7,
        scratch_shapes=[
            pltpu.VMEM((NBR, ROWS, OWN), BF16),
            pltpu.VMEM((OWN, GHOST), BF16),
            pltpu.VMEM((OWN + GHOST, GHOST), BF16),
            pltpu.VMEM((OWN + 2 * GHOST, GHOST), BF16),
            pltpu.VMEM((2, LAT, ROWS), F32),
            pltpu.VMEM((2, 8, ROWS), F32),
            pltpu.VMEM((288, ROWS), BF16),
            pltpu.VMEM((288, ROWS), BF16),
            pltpu.VMEM((NBR, LAT + 8, OWN), F32),
            pltpu.VMEM((2, NBR, LAT, OWN), F32),
            pltpu.VMEM((2, NBR, 8, OWN), F32),
            pltpu.VMEM((2, LAT, OWN), F32),
            pltpu.VMEM((2, LAT, OWN), F32),
            pltpu.VMEM((NBR, 272, OWN), BF16),
            pltpu.VMEM((LAT, OWN), F32),
            pltpu.VMEM((8, OWN), F32),
            pltpu.VMEM((LAT, ROWS), F32),
            pltpu.VMEM((8, ROWS), F32),
            pltpu.VMEM((8, OWN), F32),
            pltpu.VMEM((5, LAT, LAT), F32),
            pltpu.VMEM((LAT, 32), BF16),
            pltpu.VMEM((16, LAT), BF16),
            pltpu.VMEM((8, LAT), F32),
            pltpu.VMEM((GRAD_ROWS, LAT), F32),
            pltpu.VMEM((piece_x, LAT), F32),
            pltpu.VMEM((piece_x, LAT), F32),
            pltpu.VMEM((nz, piece_y, LAT), F32),
            pltpu.VMEM((nx - 1, piece_x, LAT), F32),
            pltpu.VMEM((ny - 1, piece_y, LAT), F32),
            pltpu.VMEM((GRAD_ROWS, LAT), F32),
            pltpu.VMEM((12, 2, MSG, GHOST), F32),
            pltpu.VMEM((12, 2, MSG, GHOST), F32),
            pltpu.SemaphoreType.DMA((12, 2)),
            pltpu.SemaphoreType.DMA((12, 2)),
            pltpu.SemaphoreType.DMA((sums,)),
            pltpu.SemaphoreType.DMA((sums,)),
        ],
        compiler_params=pltpu.CompilerParams(
            collective_id=0, has_side_effects=True, vmem_limit_bytes=48 * 1024 * 1024
        ),
        name="evolver_backward",
    )(
        latent,
        position,
        slots,
        counts,
        ghosts,
        particle_count,
        w_send,
        w_recv,
        w_geo,
        w_msg,
        w_dec,
        cot_latent,
        cot_position,
    )


def solution(mesh):
    sizes = tuple(mesh.shape[axis] for axis in AXES)
    scale = 1.0 / math.sqrt(sizes[0] * sizes[1] * sizes[2] * OWN)
    whole = P(AXES)
    rows = P(AXES, None)
    columns = P(None, AXES)
    placed = (rows, columns, whole, whole, whole, rows, rows, rows) + (P(),) * 5 + (rows, columns)
    return jax.shard_map(
        functools.partial(per_device, sizes, scale),
        mesh=mesh,
        in_specs=placed,
        out_specs=(rows, columns) + (P(),) * 5,
        check_vma=False,
    )
```

```python
import functools
import math

import jax
import jax.numpy as jnp
from jax import lax
from jax.experimental import pallas as pl
from jax.experimental.pallas import tpu as pltpu
from jax.sharding import PartitionSpec as P

MESH = pl.DeviceIdType.MESH
AXES = ("gx", "gy", "gz")
F32 = jnp.float32
BF16 = jnp.bfloat16
STRIDE = 0.1
LAT = 128
OWN = 256
NBR = 16
SIDE = 64
GHOST = 2 * SIDE
ROWS = OWN + 3 * GHOST
GRAD_ROWS = 512
MSG = SIDE + 8
UNROLL = 8
INPUTS = 15


def dot(left, right):
    return lax.dot_general(left, right, (((1,), (0,)), ((), ())), preferred_element_type=F32)


def dot_nt(left, right):
    return lax.dot_general(left, right, (((1,), (1,)), ((), ())), preferred_element_type=F32)


def split(value):
    high = value.astype(BF16)
    return high, (value - high.astype(F32)).astype(BF16)


def exact(product, left, right):
    left_high, left_low = split(left)
    right_high, right_low = split(right)
    return product(left_high, right_high) + (product(left_low, right_high) + product(left_high, right_low))


def split_rows(field_x, field_q):
    high, low = split(field_x)
    first = field_q.astype(BF16).astype(F32)
    rest = field_q - first
    second = rest.astype(BF16).astype(F32)
    third = rest - second
    upper = jnp.concatenate([first, second], axis=0).astype(BF16)
    lower = jnp.concatenate([third, jnp.zeros_like(third)], axis=0).astype(BF16)
    return high, low, upper, lower


def join_rows(product):
    value = product[0:LAT] + product[LAT : 2 * LAT]
    base = 2 * LAT
    place = product[base : base + 8] + product[base + 8 : base + 16] + product[base + 16 : base + 24]
    return value, place


def kernel(
    sizes,
    scale,
    *refs,
):
    given = refs[:INPUTS]
    out_latent_ref, out_position_ref, total = refs[INPUTS : INPUTS + 3]
    held = refs[INPUTS + 3 : 2 * INPUTS + 3]
    load_sem = refs[2 * INPUTS + 3]
    body(sizes, scale, given, held, load_sem, out_latent_ref, out_position_ref, total, *refs[2 * INPUTS + 4 :])


def body(
    sizes,
    scale,
    given,
    held,
    load_sem,
    out_latent_ref,
    out_position_ref,
    total,
    onehot,
    sel_x,
    sel_y,
    sel_z,
    tab_x,
    tab_q,
    tab_s,
    tab_a,
    gath,
    slope,
    geos,
    summed,
    fresh,
    dpre,
    d_recv,
    d_place,
    cot_x,
    cot_q,
    pad,
    w_t,
    w_geo_k,
    w_geo_s,
    d_geo,
    grads,
    part_x,
    part_y,
    part_z,
    got_x,
    got_y,
    send_buf,
    recv_buf,
    halo_send,
    halo_recv,
    sum_send,
    sum_recv,
    slots,
):
    (
        latent_ref,
        position_ref,
        particles_ref,
        count_ref,
        senders_ref,
        ghost_x_ref,
        ghost_y_ref,
        ghost_z_ref,
        w_send_ref,
        w_recv_ref,
        w_geo_ref,
        w_msg_ref,
        w_dec_ref,
        cot_latent_ref,
        cot_position_ref,
    ) = held
    ghost_refs = (ghost_x_ref, ghost_y_ref, ghost_z_ref)
    loads = [
        pltpu.make_async_copy(source, target, load_sem.at[number])
        for number, (source, target) in enumerate(zip(given, held))
    ]
    for load in loads:
        load.start()
    index = tuple(lax.axis_index(axis) for axis in AXES)
    sels = (sel_x, sel_y, sel_z)

    barrier = pltpu.get_barrier_semaphore()
    partners = 0
    for axis in range(3):
        for k in range(1, sizes[axis]):
            peer = lax.rem(index[axis] + k, sizes[axis])
            pl.semaphore_signal(barrier, inc=1, device_id={AXES[axis]: peer}, device_id_type=MESH)
            partners += 1

    lane = lax.broadcasted_iota(jnp.int32, (SIDE, GHOST), 1)
    left = lane < SIDE
    left8 = left[0:8]
    row8 = lax.broadcasted_iota(jnp.int32, (8, GHOST), 0)
    row8_own = lax.broadcasted_iota(jnp.int32, (8, OWN), 0)
    for load in loads:
        load.wait()
    live = (lax.broadcasted_iota(jnp.int32, (1, OWN), 1) < particles_ref[0]).astype(F32)

    def selector(axis):
        rows = OWN + axis * GHOST
        lists = ghost_refs[axis][...]
        chosen = jnp.concatenate([lists[0:1], lists[1:2]], axis=1)
        ids = lax.broadcasted_iota(jnp.int32, (rows, GHOST), 0)
        sels[axis][...] = (ids == chosen).astype(F32).astype(BF16)

    pending = []

    def start_halo(phase, axis, field_x, field_q):
        turned = pltpu.roll(field_x, SIDE, 1)
        turned_q = pltpu.roll(field_q, SIDE, 1)
        send_buf[phase, 0, 0:SIDE, :] = jnp.where(left, field_x[0:SIDE], turned[SIDE:])
        send_buf[phase, 0, SIDE:MSG, :] = turned_q
        send_buf[phase, 1, 0:SIDE, :] = jnp.where(left, turned[0:SIDE], field_x[SIDE:])
        send_buf[phase, 1, SIDE:MSG, :] = turned_q
        size = sizes[axis]
        lower = lax.rem(index[axis] + size - 1, size)
        upper = lax.rem(index[axis] + 1, size)
        copies = []
        for side, peer in ((0, lower), (1, upper)):
            copy = pltpu.make_async_remote_copy(
                src_ref=send_buf.at[phase, side],
                dst_ref=recv_buf.at[phase, 1 - side],
                send_sem=halo_send.at[phase, side],
                recv_sem=halo_recv.at[phase, 1 - side],
                device_id={AXES[axis]: peer},
                device_id_type=MESH,
            )
            copy.start()
            copies.append(copy)
        pending.extend(copies)
        return copies

    def end_halo(phase, copies):
        for copy in copies:
            copy.wait_recv()
        before = recv_buf[phase, 0, 0:SIDE, :]
        after = recv_buf[phase, 1, 0:SIDE, :]
        top = jnp.where(left, before, pltpu.roll(after, SIDE, 1))
        bottom = jnp.where(left, pltpu.roll(before, SIDE, 1), after)
        field_q = jnp.where(left8, recv_buf[phase, 0, SIDE:MSG, :], recv_buf[phase, 1, SIDE:MSG, :])
        return jnp.concatenate([top, bottom], axis=0), field_q

    def set_block(step, start, width, field_x, field_q):
        cols = slice(start, start + width)
        tab_x[step, :, cols] = field_x
        tab_q[step, :, cols] = field_q
        high, low, upper, lower = split_rows(field_x, field_q)
        tab_s[0:LAT, cols] = high
        tab_s[LAT : 2 * LAT, cols] = low
        tab_s[256:272, cols] = upper
        tab_s[272:288, cols] = lower

    def project_block(step, start, width):
        cols = slice(start, start + width)
        high, low = split(exact(dot, w_t[0], tab_x[step, :, cols]))
        tab_a[0:LAT, cols] = high
        tab_a[LAT : 2 * LAT, cols] = low
        tab_a[256:288, cols] = tab_s[256:288, cols]

    def select(axis, start, width):
        return dot(tab_s[:, start : start + width], sels[axis][start : start + width, :])

    def send_rows(phase, axis, product):
        field_x, field_q = join_rows(product)
        low = jnp.where(index[axis] == 0, float(sizes[axis]), 0.0)
        high = jnp.where(index[axis] == sizes[axis] - 1, -float(sizes[axis]), 0.0)
        offset = jnp.where(row8 == axis, jnp.where(left8, low, high), 0.0)
        return start_halo(phase, axis, field_x, field_q + offset)

    def gather_block(start, width, extra=None):
        def body(n, carry):
            value, place = join_rows(dot(tab_a[:, start : start + width], onehot[n, start : start + width, :]))
            if extra is None:
                gath[n, 0:LAT, :] += value
                gath[n, LAT:, :] += place
            else:
                gath[n, 0:LAT, :] = value + extra[...]
                gath[n, LAT:, :] = place
            return carry

        lax.fori_loop(0, NBR, body, 0, unroll=UNROLL)

    def forward(step, phase, prologue):
        copies = send_rows(phase, 0, select(0, 0, OWN))
        prologue()
        project_block(step, 0, OWN)
        d_recv[...] = exact(dot, w_t[1], tab_x[step, :, 0:OWN])
        early_y = select(1, 0, OWN)
        early_z = select(2, 0, OWN)
        gather_block(0, OWN, d_recv)
        start = OWN
        set_block(step, start, GHOST, *end_halo(phase, copies))
        copies = send_rows(phase + 1, 1, early_y + select(1, start, GHOST))
        early_z = early_z + select(2, start, GHOST)
        project_block(step, start, GHOST)
        gather_block(start, GHOST)
        start = start + GHOST
        set_block(step, start, GHOST, *end_halo(phase + 1, copies))
        copies = send_rows(phase + 2, 2, early_z + select(2, start, GHOST))
        project_block(step, start, GHOST)
        gather_block(start, GHOST)
        start = start + GHOST
        set_block(step, start, GHOST, *end_halo(phase + 2, copies))
        project_block(step, start, GHOST)
        own_q = tab_q[step, :, 0:OWN]
        counts = count_ref[...]
        summed[step] = jnp.zeros((LAT, OWN), F32)

        def body(n, carry):
            value, place = join_rows(dot(tab_a[:, start : start + GHOST], onehot[n, start : start + GHOST, :]))
            rel = gath[n, LAT:, :] + place - own_q
            dist = jnp.sum(rel * rel, axis=0, keepdims=True)
            geo = jnp.where(row8_own == 3, dist, rel)
            geos[step, n] = geo
            coarse = geo.astype(BF16).astype(F32)
            fine = geo - coarse
            rows = jnp.concatenate([coarse, fine, coarse, jnp.zeros_like(fine)], axis=0).astype(BF16)
            pre = gath[n, 0:LAT, :] + value + dot(w_geo_k[...], rows)
            gate = 0.5 * jnp.tanh(0.5 * pre) + 0.5
            keep = (counts > n).astype(F32)
            gate_keep = gate * keep
            summed[step] += pre * gate_keep
            slope[step, n] = gate_keep * (1.0 + pre * (1.0 - gate))
            return carry

        lax.fori_loop(0, NBR, body, 0, unroll=UNROLL)
        new_x = tab_x[step, :, 0:OWN] + live * exact(dot, w_t[2], summed[step])
        fresh[step] = new_x
        return new_x

    def scatter(start, width):
        def body(n, carry):
            return carry + dot_nt(dpre[n], onehot[n, start : start + width, :])

        product = lax.fori_loop(0, NBR, body, jnp.zeros((272, width), F32), unroll=UNROLL)
        return product[0:LAT] + product[LAT : 2 * LAT], product[256:264] + product[264:272]

    def backward(step, phase, cot_v, cot_p, first, tail):
        move = STRIDE * live * cot_p
        full = cot_v
        for k in range(3):
            full = full + w_t[3, :, k : k + 1] * move[k : k + 1, :]
        d_agg = live * full
        d_sum = exact(dot, w_msg_ref[...], d_agg)
        d_recv[...] = jnp.zeros((LAT, OWN), F32)
        d_place[...] = jnp.zeros((8, OWN), F32)
        d_geo[...] = jnp.zeros((8, LAT), F32)

        def body(n, carry):
            value = d_sum * slope[step, n]
            geo = geos[step, n]
            high, low = split(value)
            dpre[n, 0:LAT, :] = high
            dpre[n, LAT : 2 * LAT, :] = low
            d_recv[...] += value
            main = dot(w_geo_s[...], high)
            side = dot(w_geo_s[...], low)
            back = main[0:8] + main[8:16] + side[0:8]
            d_rel = jnp.where(row8_own < 3, back + 2.0 * geo * back[3:4], 0.0)
            d_place[...] -= d_rel
            coarse = d_rel.astype(BF16).astype(F32)
            dpre[n, 256:272, :] = jnp.concatenate([coarse, d_rel - coarse], axis=0).astype(BF16)
            geo_high = geo.astype(BF16).astype(F32)
            geo_rows = jnp.concatenate([geo_high, geo - geo_high], axis=0).astype(BF16)
            main = dot_nt(geo_rows, high)
            side = dot_nt(geo_rows, low)
            d_geo[...] += main[0:8] + main[8:16] + side[0:8]
            return carry

        lax.fori_loop(0, NBR, body, 0, unroll=UNROLL)

        start = OWN + 2 * GHOST
        d_send, d_q = scatter(start, GHOST)
        copies = start_halo(phase, 2, exact(dot, w_send_ref[...], d_send), d_q)
        d_weight = exact(dot_nt, tab_x[step, :, start : start + GHOST], d_send)
        for start, width in ((OWN + GHOST, GHOST), (OWN, GHOST), (0, OWN)):
            d_send, d_q = scatter(start, width)
            cot_x[:, start : start + width] = exact(dot, w_send_ref[...], d_send)
            cot_q[:, start : start + width] = d_q
            d_weight = d_weight + exact(dot_nt, tab_x[step, :, start : start + width], d_send)
        cot_x[:, 0:OWN] += full + exact(dot, w_recv_ref[...], d_recv[...])
        cot_q[:, 0:OWN] += cot_p + d_place[...]
        pieces = (
            (0, LAT, d_weight),
            (LAT, LAT, exact(dot_nt, tab_x[step, :, 0:OWN], d_recv[...])),
            (2 * LAT, LAT, exact(dot_nt, summed[step], d_agg)),
            (3 * LAT, 8, d_geo[...]),
            (3 * LAT + 8, 8, exact(dot_nt, move, fresh[step])),
        )
        for base, rows, piece in pieces:
            if first:
                grads[base : base + rows, :] = piece
            else:
                grads[base : base + rows, :] += piece
        tail(0)

        def arrived(number, axis, copies):
            field_x, field_q = end_halo(number, copies)
            high, low = split(field_x)
            coarse = field_q.astype(BF16).astype(F32)
            rows = jnp.concatenate([coarse, field_q - coarse], axis=0).astype(BF16)

            def add(start, width):
                sel = sels[axis][start : start + width, :]
                extra = dot_nt(high, sel) + dot_nt(low, sel)
                extra_q = dot_nt(rows, sel)
                cot_x[:, start : start + width] += extra
                cot_q[:, start : start + width] += extra_q[0:8] + extra_q[8:16]

            return add

        add = arrived(phase, 2, copies)
        start = OWN + GHOST
        add(start, GHOST)
        copies = start_halo(phase + 1, 1, cot_x[:, start : start + GHOST], cot_q[:, start : start + GHOST])
        add(OWN, GHOST)
        add(0, OWN)
        add = arrived(phase + 1, 1, copies)
        start = OWN
        add(start, GHOST)
        copies = start_halo(phase + 2, 0, cot_x[:, start : start + GHOST], cot_q[:, start : start + GHOST])
        add(0, OWN)
        tail(1)
        add = arrived(phase + 2, 0, copies)
        add(0, OWN)
        return cot_x[:, 0:OWN], cot_q[:, 0:OWN]

    pad[...] = jnp.zeros((8, OWN), F32)
    pad[0:3, :] = position_ref[...]
    set_block(0, 0, OWN, jnp.transpose(latent_ref[...]), pad[...])
    selector(0)
    pl.semaphore_wait(barrier, partners)

    def prologue():
        selector(1)
        selector(2)
        w_t[0] = jnp.transpose(w_send_ref[...])
        w_t[1] = jnp.transpose(w_recv_ref[...])
        w_t[2] = jnp.transpose(w_msg_ref[...])
        w_t[3] = jnp.zeros((LAT, LAT), F32)
        w_t[3, 0:3, :] = w_dec_ref[...]
        w_t[3] = jnp.transpose(w_t[3])
        w_t[4] = jnp.zeros((LAT, LAT), F32)
        w_t[4, 0:4, :] = w_geo_ref[...]
        w_geo = w_t[4, 0:8, :]
        coarse = w_geo.astype(BF16).astype(F32)
        fine = w_geo - coarse
        w_geo_s[...] = jnp.concatenate([coarse, fine], axis=0).astype(BF16)
        w_t[4, 0:8, :] = coarse
        w_t[4, 8:16, :] = coarse
        w_t[4, 16:24, :] = fine
        w_geo_k[...] = jnp.transpose(w_t[4])[:, 0:32].astype(BF16)
        grads[...] = jnp.zeros((GRAD_ROWS, LAT), F32)

        flat = senders_ref[...]
        spread = jnp.broadcast_to(flat[:, None, :], (OWN // 8, 8, LAT)).reshape(OWN, LAT)
        lanes = lax.broadcasted_iota(jnp.int32, (OWN, LAT), 1)
        sublanes = lax.broadcasted_iota(jnp.int32, (OWN, LAT), 0)
        mine = lanes // NBR == sublanes % 8
        rest = spread % 8
        slot = lax.broadcasted_iota(jnp.int32, (NBR, LAT), 1) % NBR == lax.broadcasted_iota(jnp.int32, (NBR, LAT), 0)
        slot = slot.astype(F32).astype(BF16)
        coarse = jnp.where(mine, spread - rest, 0).astype(F32).astype(BF16)
        fine = jnp.where(mine, rest, 0).astype(F32).astype(BF16)
        slots[...] = (dot_nt(slot, coarse) + dot_nt(slot, fine)).astype(jnp.int32)

        def body(n, carry):
            ids = lax.broadcasted_iota(jnp.int32, (ROWS, OWN), 0)
            onehot[n] = (ids == slots[pl.ds(n, 1), :]).astype(F32).astype(BF16)
            return carry

        lax.fori_loop(0, NBR, body, 0)

    new_x = forward(0, 0, prologue)
    w_dec = jnp.concatenate([w_dec_ref[...], jnp.zeros((5, LAT), F32)], axis=0)
    new_q = tab_q[0, :, 0:OWN] + STRIDE * live * exact(dot, w_dec, new_x)
    set_block(1, 0, OWN, new_x, new_q)
    forward(1, 3, lambda: None)

    pad[0:3, :] = cot_position_ref[...]
    cot_v, cot_p = backward(1, 6, jnp.transpose(cot_latent_ref[...]), pad[...], True, lambda number: None)

    piece_x = GRAD_ROWS // sizes[0]
    piece_y = piece_x // sizes[1]
    bases = (0, sizes[0] - 1, sizes[0] + sizes[1] - 2)
    more = bases[2] + sizes[2] - 1

    def exchange(axis, base, source, target):
        copies = []
        for k in range(1, sizes[axis]):
            peer = lax.rem(index[axis] + k, sizes[axis])
            copy = pltpu.make_async_remote_copy(
                src_ref=source(peer),
                dst_ref=target(k),
                send_sem=sum_send.at[base + k - 1],
                recv_sem=sum_recv.at[base + k - 1],
                device_id={AXES[axis]: peer},
                device_id_type=MESH,
            )
            copy.start()
            copies.append(copy)
        pending.extend(copies)
        return copies

    state = {}

    def tail(number):
        if number == 0:
            state["x"] = exchange(
                0,
                bases[0],
                lambda peer: grads.at[pl.ds(pl.multiple_of(peer * piece_x, 8), piece_x), :],
                lambda k: got_x.at[k - 1],
            )
        else:
            for copy in state["x"]:
                copy.wait_recv()
            value = grads[pl.ds(pl.multiple_of(index[0] * piece_x, 8), piece_x), :]
            for k in range(sizes[0] - 1):
                value = value + got_x[k]
            part_x[...] = value
            state["y"] = exchange(
                1,
                bases[1],
                lambda peer: part_x.at[pl.ds(pl.multiple_of(peer * piece_y, 8), piece_y), :],
                lambda k: got_y.at[k - 1],
            )

    cot_v, cot_p = backward(0, 9, cot_v, cot_p, False, tail)
    for copy in state["y"]:
        copy.wait_recv()
    value = part_x[pl.ds(pl.multiple_of(index[1] * piece_y, 8), piece_y), :]
    for k in range(sizes[1] - 1):
        value = value + got_y[k]
    part_z[index[2]] = value
    copies = exchange(2, bases[2], lambda peer: part_z.at[index[2]], lambda k: part_z.at[index[2]])
    out_latent_ref[...] = jnp.transpose(cot_v)
    out_position_ref[...] = cot_p[0:3]
    for copy in copies:
        copy.wait_recv()
    value = part_z[0]
    for k in range(1, sizes[2]):
        value = value + part_z[k]
    own_y = pl.ds(pl.multiple_of(index[1] * piece_y, 8), piece_y)
    part_y[own_y, :] = value * scale
    copies = exchange(1, more, lambda peer: part_y.at[own_y, :], lambda k: part_y.at[own_y, :])
    for copy in copies:
        copy.wait_recv()
    own_x = pl.ds(pl.multiple_of(index[0] * piece_x, 8), piece_x)
    total[own_x, :] = part_y[...]
    copies = exchange(0, more + sizes[1] - 1, lambda peer: part_y, lambda k: total.at[own_x, :])
    for copy in copies:
        copy.wait_recv()
    for copy in pending:
        copy.wait_send()


def hand_out(grad_x, grad_q, total, out_x, out_q, out_send, out_recv, out_geo, out_msg, out_dec, sems):
    pairs = (
        (grad_x, out_x),
        (grad_q, out_q),
        (total.at[0:LAT, :], out_send),
        (total.at[LAT : 2 * LAT, :], out_recv),
        (total.at[3 * LAT : 3 * LAT + 4, :], out_geo),
        (total.at[2 * LAT : 3 * LAT, :], out_msg),
        (total.at[3 * LAT + 8 : 3 * LAT + 11, :], out_dec),
    )
    copies = [pltpu.make_async_copy(source, target, sems.at[n]) for n, (source, target) in enumerate(pairs)]
    for copy in copies:
        copy.start()
    for copy in copies:
        copy.wait()


def per_device(sizes, scale, *args):
    (
        latent,
        position,
        particle_count,
        nbr_count,
        senders,
        ghost_x,
        ghost_y,
        ghost_z,
        w_send,
        w_recv,
        w_geo,
        w_msg,
        w_dec,
        cot_latent,
        cot_position,
    ) = args
    given = (
        latent,
        position,
        particle_count,
        nbr_count.reshape(1, OWN),
        senders.reshape(OWN * NBR // LAT, LAT),
        ghost_x,
        ghost_y,
        ghost_z,
        w_send,
        w_recv,
        w_geo,
        w_msg,
        w_dec,
        cot_latent,
        cot_position,
    )
    nx, ny, nz = sizes
    piece_x = GRAD_ROWS // nx
    piece_y = piece_x // ny
    sums = 2 * (nx - 1) + 2 * (ny - 1) + (nz - 1)
    vmem = pl.BlockSpec(memory_space=pltpu.VMEM)
    anywhere = pl.BlockSpec(memory_space=pl.ANY)
    held = [(pltpu.SMEM if array.size == 1 else pltpu.VMEM)(array.shape, array.dtype) for array in given]
    grad_x, grad_q, total = pl.pallas_call(
        functools.partial(kernel, sizes, scale),
        out_shape=(
            jax.ShapeDtypeStruct((OWN, LAT), F32),
            jax.ShapeDtypeStruct((3, OWN), F32),
            jax.ShapeDtypeStruct((GRAD_ROWS, LAT), F32),
        ),
        in_specs=[pl.BlockSpec(memory_space=pltpu.HBM)] * INPUTS,
        out_specs=(vmem,) * 3,
        scratch_shapes=[
            *held,
            pltpu.SemaphoreType.DMA((INPUTS,)),
            pltpu.VMEM((NBR, ROWS, OWN), BF16),
            pltpu.VMEM((OWN, GHOST), BF16),
            pltpu.VMEM((OWN + GHOST, GHOST), BF16),
            pltpu.VMEM((OWN + 2 * GHOST, GHOST), BF16),
            pltpu.VMEM((2, LAT, ROWS), F32),
            pltpu.VMEM((2, 8, ROWS), F32),
            pltpu.VMEM((288, ROWS), BF16),
            pltpu.VMEM((288, ROWS), BF16),
            pltpu.VMEM((NBR, LAT + 8, OWN), F32),
            pltpu.VMEM((2, NBR, LAT, OWN), F32),
            pltpu.VMEM((2, NBR, 8, OWN), F32),
            pltpu.VMEM((2, LAT, OWN), F32),
            pltpu.VMEM((2, LAT, OWN), F32),
            pltpu.VMEM((NBR, 272, OWN), BF16),
            pltpu.VMEM((LAT, OWN), F32),
            pltpu.VMEM((8, OWN), F32),
            pltpu.VMEM((LAT, ROWS), F32),
            pltpu.VMEM((8, ROWS), F32),
            pltpu.VMEM((8, OWN), F32),
            pltpu.VMEM((5, LAT, LAT), F32),
            pltpu.VMEM((LAT, 32), BF16),
            pltpu.VMEM((16, LAT), BF16),
            pltpu.VMEM((8, LAT), F32),
            pltpu.VMEM((GRAD_ROWS, LAT), F32),
            pltpu.VMEM((piece_x, LAT), F32),
            pltpu.VMEM((piece_x, LAT), F32),
            pltpu.VMEM((nz, piece_y, LAT), F32),
            pltpu.VMEM((nx - 1, piece_x, LAT), F32),
            pltpu.VMEM((ny - 1, piece_y, LAT), F32),
            pltpu.VMEM((12, 2, MSG, GHOST), F32),
            pltpu.VMEM((12, 2, MSG, GHOST), F32),
            pltpu.SemaphoreType.DMA((12, 2)),
            pltpu.SemaphoreType.DMA((12, 2)),
            pltpu.SemaphoreType.DMA((sums,)),
            pltpu.SemaphoreType.DMA((sums,)),
            pltpu.VMEM((NBR, OWN), jnp.int32),
        ],
        compiler_params=pltpu.CompilerParams(
            collective_id=0, has_side_effects=True, vmem_limit_bytes=64 * 1024 * 1024
        ),
        name="evolver_backward",
    )(*given)
    return pl.pallas_call(
        hand_out,
        out_shape=(
            jax.ShapeDtypeStruct((OWN, LAT), F32),
            jax.ShapeDtypeStruct((3, OWN), F32),
            jax.ShapeDtypeStruct((LAT, LAT), F32),
            jax.ShapeDtypeStruct((LAT, LAT), F32),
            jax.ShapeDtypeStruct((4, LAT), F32),
            jax.ShapeDtypeStruct((LAT, LAT), F32),
            jax.ShapeDtypeStruct((3, LAT), F32),
        ),
        in_specs=[vmem] * 3,
        out_specs=(anywhere,) * 7,
        scratch_shapes=[pltpu.SemaphoreType.DMA((7,))],
        name="hand_out",
    )(grad_x, grad_q, total)


def solution(mesh):
    sizes = tuple(mesh.shape[axis] for axis in AXES)
    scale = 1.0 / math.sqrt(sizes[0] * sizes[1] * sizes[2] * OWN)
    whole = P(AXES)
    rows = P(AXES, None)
    columns = P(None, AXES)
    placed = (rows, columns, whole, whole, whole, rows, rows, rows) + (P(),) * 5 + (rows, columns)
    return jax.shard_map(
        functools.partial(per_device, sizes, scale),
        mesh=mesh,
        in_specs=placed,
        out_specs=(rows, columns) + (P(),) * 5,
        check_vma=False,
    )
```

```python
import functools
import math

import jax
import jax.numpy as jnp
from jax import lax
from jax.experimental import pallas as pl
from jax.experimental.pallas import tpu as pltpu
from jax.sharding import PartitionSpec as P

MESH = pl.DeviceIdType.MESH
AXES = ("gx", "gy", "gz")
F32 = jnp.float32
BF16 = jnp.bfloat16
STRIDE = 0.1
LAT = 128
OWN = 256
NBR = 16
SIDE = 64
GHOST = 2 * SIDE
ROWS = OWN + 3 * GHOST
GRAD_ROWS = 512
MSG = SIDE + 8
UNROLL = 8
INPUTS = 15
CORES = 2
LOWS = 2


def dot(left, right):
    return lax.dot_general(left, right, (((1,), (0,)), ((), ())), preferred_element_type=F32)


def dot_nt(left, right):
    return lax.dot_general(left, right, (((1,), (1,)), ((), ())), preferred_element_type=F32)


def split(value):
    high = value.astype(BF16)
    return high, (value - high.astype(F32)).astype(BF16)


def exact(product, left, right):
    left_high, left_low = split(left)
    right_high, right_low = split(right)
    return product(left_high, right_high) + (product(left_low, right_high) + product(left_high, right_low))


def split_rows(field_x, field_q):
    high, low = split(field_x)
    first = field_q.astype(BF16).astype(F32)
    rest = field_q - first
    second = rest.astype(BF16).astype(F32)
    third = rest - second
    upper = jnp.concatenate([first, second], axis=0).astype(BF16)
    lower = jnp.concatenate([third, jnp.zeros_like(third)], axis=0).astype(BF16)
    return high, low, upper, lower


def join_rows(product):
    value = product[0:LAT] + product[LAT : 2 * LAT]
    base = 2 * LAT
    place = product[base : base + 8] + product[base + 8 : base + 16] + product[base + 16 : base + 24]
    return value, place


def kernel(
    sizes,
    scale,
    *refs,
):
    given = refs[:INPUTS]
    out_latent_ref, out_position_ref, total = refs[INPUTS : INPUTS + 3]
    held = refs[INPUTS + 3 : 2 * INPUTS + 3]
    load_sem = refs[2 * INPUTS + 3]
    body(sizes, scale, given, held, load_sem, out_latent_ref, out_position_ref, total, *refs[2 * INPUTS + 4 :])


def body(
    sizes,
    scale,
    given,
    held,
    load_sem,
    out_latent_ref,
    out_position_ref,
    total,
    onehot,
    sel_x,
    sel_y,
    sel_z,
    tab_x,
    tab_q,
    tab_s,
    tab_a,
    gath,
    slope,
    geos,
    summed,
    fresh,
    dpre,
    d_recv,
    d_place,
    cot_x,
    cot_q,
    pad,
    w_t,
    w_geo_k,
    w_geo_s,
    d_geo,
    grads,
    part_half,
    part_ring,
    got_core,
    got_plane,
    send_buf,
    recv_buf,
    halo_send,
    halo_recv,
    sum_send,
    sum_recv,
    slots,
):
    (
        latent_ref,
        position_ref,
        particles_ref,
        count_ref,
        senders_ref,
        ghost_x_ref,
        ghost_y_ref,
        ghost_z_ref,
        w_send_ref,
        w_recv_ref,
        w_geo_ref,
        w_msg_ref,
        w_dec_ref,
        cot_latent_ref,
        cot_position_ref,
    ) = held
    ghost_refs = (ghost_x_ref, ghost_y_ref, ghost_z_ref)
    loads = [
        pltpu.make_async_copy(source, target, load_sem.at[number])
        for number, (source, target) in enumerate(zip(given, held))
    ]
    for load in loads:
        load.start()
    index = tuple(lax.axis_index(axis) for axis in AXES)
    sels = (sel_x, sel_y, sel_z)

    barrier = pltpu.get_barrier_semaphore()
    core, y = lax.rem(index[0], CORES), lax.div(index[0], CORES)
    lows, xs = LOWS, sizes[1] // LOWS
    x, low = lax.rem(index[1], xs), lax.div(index[1], xs)
    plane, ring = sizes[0] // CORES * xs, sizes[2] * lows
    at_plane, at_ring = y * xs + x, index[2] * lows + low

    def plane_peer(k):
        place = lax.rem(at_plane + k, plane)
        return place, {"gx": lax.div(place, xs) * CORES + core, "gy": low * xs + lax.rem(place, xs)}

    def ring_peer(k):
        place = lax.rem(at_ring + k, ring)
        return place, {"gy": lax.rem(place, lows) * xs + x, "gz": lax.div(place, lows)}

    other_core = {"gx": y * CORES + 1 - core}
    greeted = [plane_peer(k)[1] for k in range(1, plane)] + [ring_peer(k)[1] for k in range(1, ring)]
    for axis in (0, 1):
        for step in (1, sizes[axis] - 1):
            greeted.append({AXES[axis]: lax.rem(index[axis] + step, sizes[axis])})
    for peer in greeted:
        pl.semaphore_signal(barrier, inc=1, device_id=peer, device_id_type=MESH)
    partners = len(greeted)

    lane = lax.broadcasted_iota(jnp.int32, (SIDE, GHOST), 1)
    left = lane < SIDE
    left8 = left[0:8]
    row8 = lax.broadcasted_iota(jnp.int32, (8, GHOST), 0)
    row8_own = lax.broadcasted_iota(jnp.int32, (8, OWN), 0)
    for load in loads:
        load.wait()
    live = (lax.broadcasted_iota(jnp.int32, (1, OWN), 1) < particles_ref[0]).astype(F32)

    def selector(axis):
        rows = OWN + axis * GHOST
        lists = ghost_refs[axis][...]
        chosen = jnp.concatenate([lists[0:1], lists[1:2]], axis=1)
        ids = lax.broadcasted_iota(jnp.int32, (rows, GHOST), 0)
        sels[axis][...] = (ids == chosen).astype(F32).astype(BF16)

    pending = []

    def start_halo(phase, axis, field_x, field_q):
        turned = pltpu.roll(field_x, SIDE, 1)
        turned_q = pltpu.roll(field_q, SIDE, 1)
        send_buf[phase, 0, 0:SIDE, :] = jnp.where(left, field_x[0:SIDE], turned[SIDE:])
        send_buf[phase, 0, SIDE:MSG, :] = turned_q
        send_buf[phase, 1, 0:SIDE, :] = jnp.where(left, turned[0:SIDE], field_x[SIDE:])
        send_buf[phase, 1, SIDE:MSG, :] = turned_q
        size = sizes[axis]
        lower = lax.rem(index[axis] + size - 1, size)
        upper = lax.rem(index[axis] + 1, size)
        copies = []
        for side, peer in ((0, lower), (1, upper)):
            copy = pltpu.make_async_remote_copy(
                src_ref=send_buf.at[phase, side],
                dst_ref=recv_buf.at[phase, 1 - side],
                send_sem=halo_send.at[phase, side],
                recv_sem=halo_recv.at[phase, 1 - side],
                device_id={AXES[axis]: peer},
                device_id_type=MESH,
            )
            copy.start()
            copies.append(copy)
        pending.extend(copies)
        return copies

    def end_halo(phase, copies):
        for copy in copies:
            copy.wait_recv()
        before = recv_buf[phase, 0, 0:SIDE, :]
        after = recv_buf[phase, 1, 0:SIDE, :]
        top = jnp.where(left, before, pltpu.roll(after, SIDE, 1))
        bottom = jnp.where(left, pltpu.roll(before, SIDE, 1), after)
        field_q = jnp.where(left8, recv_buf[phase, 0, SIDE:MSG, :], recv_buf[phase, 1, SIDE:MSG, :])
        return jnp.concatenate([top, bottom], axis=0), field_q

    def set_block(step, start, width, field_x, field_q):
        cols = slice(start, start + width)
        tab_x[step, :, cols] = field_x
        tab_q[step, :, cols] = field_q
        high, low, upper, lower = split_rows(field_x, field_q)
        tab_s[0:LAT, cols] = high
        tab_s[LAT : 2 * LAT, cols] = low
        tab_s[256:272, cols] = upper
        tab_s[272:288, cols] = lower

    def project_block(step, start, width):
        cols = slice(start, start + width)
        high, low = split(exact(dot, w_t[0], tab_x[step, :, cols]))
        tab_a[0:LAT, cols] = high
        tab_a[LAT : 2 * LAT, cols] = low
        tab_a[256:288, cols] = tab_s[256:288, cols]

    def select(axis, start, width):
        return dot(tab_s[:, start : start + width], sels[axis][start : start + width, :])

    def send_rows(phase, axis, product):
        field_x, field_q = join_rows(product)
        low = jnp.where(index[axis] == 0, float(sizes[axis]), 0.0)
        high = jnp.where(index[axis] == sizes[axis] - 1, -float(sizes[axis]), 0.0)
        offset = jnp.where(row8 == axis, jnp.where(left8, low, high), 0.0)
        return start_halo(phase, axis, field_x, field_q + offset)

    def gather_block(start, width, extra=None):
        def body(n, carry):
            value, place = join_rows(dot(tab_a[:, start : start + width], onehot[n, start : start + width, :]))
            if extra is None:
                gath[n, 0:LAT, :] += value
                gath[n, LAT:, :] += place
            else:
                gath[n, 0:LAT, :] = value + extra[...]
                gath[n, LAT:, :] = place
            return carry

        lax.fori_loop(0, NBR, body, 0, unroll=UNROLL)

    def forward(step, phase, prologue):
        copies = send_rows(phase, 0, select(0, 0, OWN))
        prologue()
        project_block(step, 0, OWN)
        d_recv[...] = exact(dot, w_t[1], tab_x[step, :, 0:OWN])
        early_y = select(1, 0, OWN)
        early_z = select(2, 0, OWN)
        gather_block(0, OWN, d_recv)
        start = OWN
        set_block(step, start, GHOST, *end_halo(phase, copies))
        copies = send_rows(phase + 1, 1, early_y + select(1, start, GHOST))
        early_z = early_z + select(2, start, GHOST)
        project_block(step, start, GHOST)
        gather_block(start, GHOST)
        start = start + GHOST
        set_block(step, start, GHOST, *end_halo(phase + 1, copies))
        copies = send_rows(phase + 2, 2, early_z + select(2, start, GHOST))
        project_block(step, start, GHOST)
        gather_block(start, GHOST)
        start = start + GHOST
        set_block(step, start, GHOST, *end_halo(phase + 2, copies))
        project_block(step, start, GHOST)
        own_q = tab_q[step, :, 0:OWN]
        counts = count_ref[...]
        summed[step] = jnp.zeros((LAT, OWN), F32)

        def body(n, carry):
            value, place = join_rows(dot(tab_a[:, start : start + GHOST], onehot[n, start : start + GHOST, :]))
            rel = gath[n, LAT:, :] + place - own_q
            dist = jnp.sum(rel * rel, axis=0, keepdims=True)
            geo = jnp.where(row8_own == 3, dist, rel)
            geos[step, n] = geo
            coarse = geo.astype(BF16).astype(F32)
            fine = geo - coarse
            rows = jnp.concatenate([coarse, fine, coarse, jnp.zeros_like(fine)], axis=0).astype(BF16)
            pre = gath[n, 0:LAT, :] + value + dot(w_geo_k[...], rows)
            gate = 0.5 * jnp.tanh(0.5 * pre) + 0.5
            keep = (counts > n).astype(F32)
            gate_keep = gate * keep
            summed[step] += pre * gate_keep
            slope[step, n] = gate_keep * (1.0 + pre * (1.0 - gate))
            return carry

        lax.fori_loop(0, NBR, body, 0, unroll=UNROLL)
        new_x = tab_x[step, :, 0:OWN] + live * exact(dot, w_t[2], summed[step])
        fresh[step] = new_x
        return new_x

    def scatter(start, width):
        def body(n, carry):
            return carry + dot_nt(dpre[n], onehot[n, start : start + width, :])

        product = lax.fori_loop(0, NBR, body, jnp.zeros((272, width), F32), unroll=UNROLL)
        return product[0:LAT] + product[LAT : 2 * LAT], product[256:264] + product[264:272]

    def backward(step, phase, cot_v, cot_p, first, tail):
        move = STRIDE * live * cot_p
        full = cot_v
        for k in range(3):
            full = full + w_t[3, :, k : k + 1] * move[k : k + 1, :]
        d_agg = live * full
        d_sum = exact(dot, w_msg_ref[...], d_agg)
        d_recv[...] = jnp.zeros((LAT, OWN), F32)
        d_place[...] = jnp.zeros((8, OWN), F32)
        d_geo[...] = jnp.zeros((8, LAT), F32)

        def body(n, carry):
            value = d_sum * slope[step, n]
            geo = geos[step, n]
            high, low = split(value)
            dpre[n, 0:LAT, :] = high
            dpre[n, LAT : 2 * LAT, :] = low
            d_recv[...] += value
            main = dot(w_geo_s[...], high)
            side = dot(w_geo_s[...], low)
            back = main[0:8] + main[8:16] + side[0:8]
            d_rel = jnp.where(row8_own < 3, back + 2.0 * geo * back[3:4], 0.0)
            d_place[...] -= d_rel
            coarse = d_rel.astype(BF16).astype(F32)
            dpre[n, 256:272, :] = jnp.concatenate([coarse, d_rel - coarse], axis=0).astype(BF16)
            geo_high = geo.astype(BF16).astype(F32)
            geo_rows = jnp.concatenate([geo_high, geo - geo_high], axis=0).astype(BF16)
            main = dot_nt(geo_rows, high)
            side = dot_nt(geo_rows, low)
            d_geo[...] += main[0:8] + main[8:16] + side[0:8]
            return carry

        lax.fori_loop(0, NBR, body, 0, unroll=UNROLL)

        start = OWN + 2 * GHOST
        d_send, d_q = scatter(start, GHOST)
        if first:
            copies = start_halo(phase, 2, exact(dot, w_send_ref[...], d_send), d_q)
        else:
            ghost_x, ghost_q = exact(dot, w_send_ref[...], d_send), d_q
        d_weight = exact(dot_nt, tab_x[step, :, start : start + GHOST], d_send)
        for start, width in ((OWN + GHOST, GHOST), (OWN, GHOST), (0, OWN)):
            d_send, d_q = scatter(start, width)
            cot_x[:, start : start + width] = exact(dot, w_send_ref[...], d_send)
            cot_q[:, start : start + width] = d_q
            d_weight = d_weight + exact(dot_nt, tab_x[step, :, start : start + width], d_send)
        cot_x[:, 0:OWN] += full + exact(dot, w_recv_ref[...], d_recv[...])
        cot_q[:, 0:OWN] += cot_p + d_place[...]
        pieces = (
            (0, LAT, d_weight),
            (LAT, LAT, exact(dot_nt, tab_x[step, :, 0:OWN], d_recv[...])),
            (2 * LAT, LAT, exact(dot_nt, summed[step], d_agg)),
            (3 * LAT, 8, d_geo[...]),
            (3 * LAT + 8, 8, exact(dot_nt, move, fresh[step])),
        )
        for base, rows, piece in pieces:
            if first:
                grads[base : base + rows, :] = piece
            else:
                grads[base : base + rows, :] += piece
        tail(0)
        if not first:
            copies = start_halo(phase, 2, ghost_x, ghost_q)
        tail(1)

        def arrived(number, axis, copies):
            field_x, field_q = end_halo(number, copies)
            high, low = split(field_x)
            coarse = field_q.astype(BF16).astype(F32)
            rows = jnp.concatenate([coarse, field_q - coarse], axis=0).astype(BF16)

            def add(start, width):
                sel = sels[axis][start : start + width, :]
                extra = dot_nt(high, sel) + dot_nt(low, sel)
                extra_q = dot_nt(rows, sel)
                cot_x[:, start : start + width] += extra
                cot_q[:, start : start + width] += extra_q[0:8] + extra_q[8:16]

            return add

        add = arrived(phase, 2, copies)
        start = OWN + GHOST
        add(start, GHOST)
        copies = start_halo(phase + 1, 1, cot_x[:, start : start + GHOST], cot_q[:, start : start + GHOST])
        add(OWN, GHOST)
        add(0, OWN)
        tail(2)
        add = arrived(phase + 1, 1, copies)
        start = OWN
        add(start, GHOST)
        copies = start_halo(phase + 2, 0, cot_x[:, start : start + GHOST], cot_q[:, start : start + GHOST])
        add(0, OWN)
        tail(3)
        add = arrived(phase + 2, 0, copies)
        add(0, OWN)
        return cot_x[:, 0:OWN], cot_q[:, 0:OWN]

    pad[...] = jnp.zeros((8, OWN), F32)
    pad[0:3, :] = position_ref[...]
    set_block(0, 0, OWN, jnp.transpose(latent_ref[...]), pad[...])
    selector(0)
    pl.semaphore_wait(barrier, partners)

    def prologue():
        selector(1)
        selector(2)
        w_t[0] = jnp.transpose(w_send_ref[...])
        w_t[1] = jnp.transpose(w_recv_ref[...])
        w_t[2] = jnp.transpose(w_msg_ref[...])
        w_t[3] = jnp.zeros((LAT, LAT), F32)
        w_t[3, 0:3, :] = w_dec_ref[...]
        w_t[3] = jnp.transpose(w_t[3])
        w_t[4] = jnp.zeros((LAT, LAT), F32)
        w_t[4, 0:4, :] = w_geo_ref[...]
        w_geo = w_t[4, 0:8, :]
        coarse = w_geo.astype(BF16).astype(F32)
        fine = w_geo - coarse
        w_geo_s[...] = jnp.concatenate([coarse, fine], axis=0).astype(BF16)
        w_t[4, 0:8, :] = coarse
        w_t[4, 8:16, :] = coarse
        w_t[4, 16:24, :] = fine
        w_geo_k[...] = jnp.transpose(w_t[4])[:, 0:32].astype(BF16)
        grads[...] = jnp.zeros((GRAD_ROWS, LAT), F32)

        flat = senders_ref[...]
        spread = jnp.broadcast_to(flat[:, None, :], (OWN // 8, 8, LAT)).reshape(OWN, LAT)
        lanes = lax.broadcasted_iota(jnp.int32, (OWN, LAT), 1)
        sublanes = lax.broadcasted_iota(jnp.int32, (OWN, LAT), 0)
        mine = lanes // NBR == sublanes % 8
        rest = spread % 8
        slot = lax.broadcasted_iota(jnp.int32, (NBR, LAT), 1) % NBR == lax.broadcasted_iota(jnp.int32, (NBR, LAT), 0)
        slot = slot.astype(F32).astype(BF16)
        coarse = jnp.where(mine, spread - rest, 0).astype(F32).astype(BF16)
        fine = jnp.where(mine, rest, 0).astype(F32).astype(BF16)
        slots[...] = (dot_nt(slot, coarse) + dot_nt(slot, fine)).astype(jnp.int32)

        def body(n, carry):
            ids = lax.broadcasted_iota(jnp.int32, (ROWS, OWN), 0)
            onehot[n] = (ids == slots[pl.ds(n, 1), :]).astype(F32).astype(BF16)
            return carry

        lax.fori_loop(0, NBR, body, 0)

    new_x = forward(0, 0, prologue)
    w_dec = jnp.concatenate([w_dec_ref[...], jnp.zeros((5, LAT), F32)], axis=0)
    new_q = tab_q[0, :, 0:OWN] + STRIDE * live * exact(dot, w_dec, new_x)
    set_block(1, 0, OWN, new_x, new_q)
    forward(1, 3, lambda: None)

    pad[0:3, :] = cot_position_ref[...]
    cot_v, cot_p = backward(1, 6, jnp.transpose(cot_latent_ref[...]), pad[...], True, lambda number: None)

    half = GRAD_ROWS // CORES
    piece = half // plane
    numbers = iter(range(2 + 2 * (plane - 1) + (ring - 1)))

    def push(source, target, peer):
        number = next(numbers)
        copy = pltpu.make_async_remote_copy(
            src_ref=source,
            dst_ref=target,
            send_sem=sum_send.at[number],
            recv_sem=sum_recv.at[number],
            device_id=peer,
            device_id_type=MESH,
        )
        copy.start()
        pending.append(copy)
        return copy

    def rows_of(base, count):
        return pl.ds(pl.multiple_of(base, 8), count)

    own_half = rows_of(core * half, half)
    own_piece = rows_of(core * half + at_plane * piece, piece)
    flying = []

    def arrive():
        for copy in flying:
            copy.wait_recv()
        flying.clear()

    def tail(number):
        if number == 0:
            flying.append(push(grads.at[rows_of((1 - core) * half, half), :], got_core, other_core))
        elif number == 1:
            arrive()
            part_half[...] = grads[own_half, :] + got_core[...]
            for k in range(1, plane):
                place, peer = plane_peer(k)
                flying.append(push(part_half.at[rows_of(place * piece, piece), :], got_plane.at[k - 1], peer))
        elif number == 2:
            arrive()
            value = part_half[rows_of(at_plane * piece, piece), :]
            for k in range(plane - 1):
                value = value + got_plane[k]
            part_ring[at_ring] = value
            for k in range(1, ring):
                flying.append(push(part_ring.at[at_ring], part_ring.at[at_ring], ring_peer(k)[1]))
        else:
            arrive()
            value = part_ring[0]
            for k in range(1, ring):
                value = value + part_ring[k]
            total[own_piece, :] = value * scale
            for k in range(1, plane):
                flying.append(push(total.at[own_piece, :], total.at[own_piece, :], plane_peer(k)[1]))

    cot_v, cot_p = backward(0, 9, cot_v, cot_p, False, tail)
    arrive()
    flying.append(push(total.at[own_half, :], total.at[own_half, :], other_core))
    out_latent_ref[...] = jnp.transpose(cot_v)
    out_position_ref[...] = cot_p[0:3]
    arrive()
    for copy in pending:
        copy.wait_send()


def hand_out(grad_x, grad_q, total, out_x, out_q, out_send, out_recv, out_geo, out_msg, out_dec, sems):
    pairs = (
        (grad_x, out_x),
        (grad_q, out_q),
        (total.at[0:LAT, :], out_send),
        (total.at[LAT : 2 * LAT, :], out_recv),
        (total.at[3 * LAT : 3 * LAT + 4, :], out_geo),
        (total.at[2 * LAT : 3 * LAT, :], out_msg),
        (total.at[3 * LAT + 8 : 3 * LAT + 11, :], out_dec),
    )
    copies = [pltpu.make_async_copy(source, target, sems.at[n]) for n, (source, target) in enumerate(pairs)]
    for copy in copies:
        copy.start()
    for copy in copies:
        copy.wait()


def per_device(sizes, scale, *args):
    (
        latent,
        position,
        particle_count,
        nbr_count,
        senders,
        ghost_x,
        ghost_y,
        ghost_z,
        w_send,
        w_recv,
        w_geo,
        w_msg,
        w_dec,
        cot_latent,
        cot_position,
    ) = args
    given = (
        latent,
        position,
        particle_count,
        nbr_count.reshape(1, OWN),
        senders.reshape(OWN * NBR // LAT, LAT),
        ghost_x,
        ghost_y,
        ghost_z,
        w_send,
        w_recv,
        w_geo,
        w_msg,
        w_dec,
        cot_latent,
        cot_position,
    )
    plane = sizes[0] // CORES * (sizes[1] // LOWS)
    ring = sizes[2] * LOWS
    half = GRAD_ROWS // CORES
    sums = 2 + 2 * (plane - 1) + (ring - 1)
    vmem = pl.BlockSpec(memory_space=pltpu.VMEM)
    anywhere = pl.BlockSpec(memory_space=pl.ANY)
    held = [(pltpu.SMEM if array.size == 1 else pltpu.VMEM)(array.shape, array.dtype) for array in given]
    grad_x, grad_q, total = pl.pallas_call(
        functools.partial(kernel, sizes, scale),
        out_shape=(
            jax.ShapeDtypeStruct((OWN, LAT), F32),
            jax.ShapeDtypeStruct((3, OWN), F32),
            jax.ShapeDtypeStruct((GRAD_ROWS, LAT), F32),
        ),
        in_specs=[pl.BlockSpec(memory_space=pltpu.HBM)] * INPUTS,
        out_specs=(vmem,) * 3,
        scratch_shapes=[
            *held,
            pltpu.SemaphoreType.DMA((INPUTS,)),
            pltpu.VMEM((NBR, ROWS, OWN), BF16),
            pltpu.VMEM((OWN, GHOST), BF16),
            pltpu.VMEM((OWN + GHOST, GHOST), BF16),
            pltpu.VMEM((OWN + 2 * GHOST, GHOST), BF16),
            pltpu.VMEM((2, LAT, ROWS), F32),
            pltpu.VMEM((2, 8, ROWS), F32),
            pltpu.VMEM((288, ROWS), BF16),
            pltpu.VMEM((288, ROWS), BF16),
            pltpu.VMEM((NBR, LAT + 8, OWN), F32),
            pltpu.VMEM((2, NBR, LAT, OWN), F32),
            pltpu.VMEM((2, NBR, 8, OWN), F32),
            pltpu.VMEM((2, LAT, OWN), F32),
            pltpu.VMEM((2, LAT, OWN), F32),
            pltpu.VMEM((NBR, 272, OWN), BF16),
            pltpu.VMEM((LAT, OWN), F32),
            pltpu.VMEM((8, OWN), F32),
            pltpu.VMEM((LAT, ROWS), F32),
            pltpu.VMEM((8, ROWS), F32),
            pltpu.VMEM((8, OWN), F32),
            pltpu.VMEM((5, LAT, LAT), F32),
            pltpu.VMEM((LAT, 32), BF16),
            pltpu.VMEM((16, LAT), BF16),
            pltpu.VMEM((8, LAT), F32),
            pltpu.VMEM((GRAD_ROWS, LAT), F32),
            pltpu.VMEM((half, LAT), F32),
            pltpu.VMEM((ring, half // plane, LAT), F32),
            pltpu.VMEM((half, LAT), F32),
            pltpu.VMEM((plane - 1, half // plane, LAT), F32),
            pltpu.VMEM((12, 2, MSG, GHOST), F32),
            pltpu.VMEM((12, 2, MSG, GHOST), F32),
            pltpu.SemaphoreType.DMA((12, 2)),
            pltpu.SemaphoreType.DMA((12, 2)),
            pltpu.SemaphoreType.DMA((sums,)),
            pltpu.SemaphoreType.DMA((sums,)),
            pltpu.VMEM((NBR, OWN), jnp.int32),
        ],
        compiler_params=pltpu.CompilerParams(
            collective_id=0, has_side_effects=True, vmem_limit_bytes=64 * 1024 * 1024
        ),
        name="evolver_backward",
    )(*given)
    return pl.pallas_call(
        hand_out,
        out_shape=(
            jax.ShapeDtypeStruct((OWN, LAT), F32),
            jax.ShapeDtypeStruct((3, OWN), F32),
            jax.ShapeDtypeStruct((LAT, LAT), F32),
            jax.ShapeDtypeStruct((LAT, LAT), F32),
            jax.ShapeDtypeStruct((4, LAT), F32),
            jax.ShapeDtypeStruct((LAT, LAT), F32),
            jax.ShapeDtypeStruct((3, LAT), F32),
        ),
        in_specs=[vmem] * 3,
        out_specs=(anywhere,) * 7,
        scratch_shapes=[pltpu.SemaphoreType.DMA((7,))],
        name="hand_out",
    )(grad_x, grad_q, total)


def solution(mesh):
    sizes = tuple(mesh.shape[axis] for axis in AXES)
    scale = 1.0 / math.sqrt(sizes[0] * sizes[1] * sizes[2] * OWN)
    whole = P(AXES)
    rows = P(AXES, None)
    columns = P(None, AXES)
    placed = (rows, columns, whole, whole, whole, rows, rows, rows) + (P(),) * 5 + (rows, columns)
    return jax.shard_map(
        functools.partial(per_device, sizes, scale),
        mesh=mesh,
        in_specs=placed,
        out_specs=(rows, columns) + (P(),) * 5,
        check_vma=False,
    )
```

```python
import functools
import math

import jax
import jax.numpy as jnp
from jax import lax
from jax.experimental import pallas as pl
from jax.experimental.pallas import tpu as pltpu
from jax.sharding import PartitionSpec as P

MESH = pl.DeviceIdType.MESH
AXES = ("gx", "gy", "gz")
F32 = jnp.float32
BF16 = jnp.bfloat16
STRIDE = 0.1
LAT = 128
OWN = 256
NBR = 16
SIDE = 64
GHOST = 2 * SIDE
ROWS = OWN + 3 * GHOST
GRAD_ROWS = 512
MSG = SIDE + 8
UNROLL = 8
INPUTS = 15
CORES = 2
LOWS = 2


def dot(left, right):
    return lax.dot_general(left, right, (((1,), (0,)), ((), ())), preferred_element_type=F32)


def dot_nt(left, right):
    return lax.dot_general(left, right, (((1,), (1,)), ((), ())), preferred_element_type=F32)


def split(value):
    high = value.astype(BF16)
    return high, (value - high.astype(F32)).astype(BF16)


def exact(left, right):
    left_high, left_low = split(left)
    right_high, right_low = split(right)
    return dot(
        jnp.concatenate([left_high, left_low, left_high], axis=1),
        jnp.concatenate([right_high, right_high, right_low], axis=0),
    )


def exact_nt(left, right):
    left_high, left_low = split(left)
    right_high, right_low = split(right)
    return dot_nt(
        jnp.concatenate([left_high, left_low, left_high], axis=1),
        jnp.concatenate([right_high, right_high, right_low], axis=1),
    )


def split_place(field_q):
    first = field_q.astype(BF16).astype(F32)
    rest = field_q - first
    second = rest.astype(BF16).astype(F32)
    third = rest - second
    left = jnp.concatenate([first, third], axis=0).astype(BF16)
    right = jnp.concatenate([second, jnp.zeros_like(third)], axis=0).astype(BF16)
    return left, right


def twice(picker):
    return jnp.concatenate([picker, picker], axis=0)


def join_rows(product):
    return product[0:LAT], product[LAT : LAT + 8] + product[LAT + 8 : LAT + 16]


def kernel(
    sizes,
    scale,
    *refs,
):
    given = refs[:INPUTS]
    out_latent_ref, out_position_ref, total = refs[INPUTS : INPUTS + 3]
    held = refs[INPUTS + 3 : 2 * INPUTS + 3]
    load_sem = refs[2 * INPUTS + 3]
    body(sizes, scale, given, held, load_sem, out_latent_ref, out_position_ref, total, *refs[2 * INPUTS + 4 :])


def body(
    sizes,
    scale,
    given,
    held,
    load_sem,
    out_latent_ref,
    out_position_ref,
    total,
    onehot,
    sel_x,
    sel_y,
    sel_z,
    back_x,
    back_y,
    back_z,
    edge_rows,
    edge_sum,
    tab_x,
    tab_q,
    tab_s,
    tab_w,
    tab_a,
    gath,
    slope,
    geos,
    summed,
    fresh,
    dpre,
    d_recv,
    d_place,
    cot_x,
    cot_q,
    pad,
    w_t,
    w_geo_k,
    w_geo_s,
    grads,
    part_half,
    part_ring,
    got_core,
    got_plane,
    send_buf,
    recv_buf,
    halo_send,
    halo_recv,
    sum_send,
    sum_recv,
    slots,
):
    (
        latent_ref,
        position_ref,
        particles_ref,
        count_ref,
        senders_ref,
        ghost_x_ref,
        ghost_y_ref,
        ghost_z_ref,
        w_send_ref,
        w_recv_ref,
        w_geo_ref,
        w_msg_ref,
        w_dec_ref,
        cot_latent_ref,
        cot_position_ref,
    ) = held
    ghost_refs = (ghost_x_ref, ghost_y_ref, ghost_z_ref)
    loads = [
        pltpu.make_async_copy(source, target, load_sem.at[number])
        for number, (source, target) in enumerate(zip(given, held))
    ]
    for load in loads:
        load.start()
    index = tuple(lax.axis_index(axis) for axis in AXES)
    sels = (sel_x, sel_y, sel_z)
    backs = (back_x, back_y, back_z)

    barrier = pltpu.get_barrier_semaphore()
    core, y = lax.rem(index[0], CORES), lax.div(index[0], CORES)
    lows, xs = LOWS, sizes[1] // LOWS
    x, low = lax.rem(index[1], xs), lax.div(index[1], xs)
    plane, ring = sizes[0] // CORES * xs, sizes[2] * lows
    at_plane, at_ring = y * xs + x, index[2] * lows + low

    def plane_peer(k):
        place = lax.rem(at_plane + k, plane)
        return place, {"gx": lax.div(place, xs) * CORES + core, "gy": low * xs + lax.rem(place, xs)}

    def ring_peer(k):
        place = lax.rem(at_ring + k, ring)
        return place, {"gy": lax.rem(place, lows) * xs + x, "gz": lax.div(place, lows)}

    other_core = {"gx": y * CORES + 1 - core}
    greeted = [plane_peer(k)[1] for k in range(1, plane)] + [ring_peer(k)[1] for k in range(1, ring)]
    for axis in (0, 1):
        for step in (1, sizes[axis] - 1):
            greeted.append({AXES[axis]: lax.rem(index[axis] + step, sizes[axis])})
    for peer in greeted:
        pl.semaphore_signal(barrier, inc=1, device_id=peer, device_id_type=MESH)
    partners = len(greeted)

    lane = lax.broadcasted_iota(jnp.int32, (SIDE, GHOST), 1)
    left = lane < SIDE
    left8 = left[0:8]
    row8 = lax.broadcasted_iota(jnp.int32, (8, GHOST), 0)
    row8_own = lax.broadcasted_iota(jnp.int32, (8, OWN), 0)
    for load in loads:
        load.wait()
    live = (lax.broadcasted_iota(jnp.int32, (1, OWN), 1) < particles_ref[0]).astype(F32)

    def selector(axis):
        rows = OWN + axis * GHOST
        lists = ghost_refs[axis][...]
        chosen = jnp.concatenate([lists[0:1], lists[1:2]], axis=1)
        ids = lax.broadcasted_iota(jnp.int32, (rows, GHOST), 0)
        picked = (ids == chosen).astype(F32)
        sels[axis][...] = picked.astype(BF16)
        return picked

    def edges_of(n):
        return pl.ds(pl.multiple_of(n * OWN, OWN), OWN)

    pending = []

    def start_halo(phase, axis, field_x, field_q):
        turned = pltpu.roll(field_x, SIDE, 1)
        turned_q = pltpu.roll(field_q, SIDE, 1)
        send_buf[phase, 0, 0:SIDE, :] = jnp.where(left, field_x[0:SIDE], turned[SIDE:])
        send_buf[phase, 0, SIDE:MSG, :] = turned_q
        send_buf[phase, 1, 0:SIDE, :] = jnp.where(left, turned[0:SIDE], field_x[SIDE:])
        send_buf[phase, 1, SIDE:MSG, :] = turned_q
        size = sizes[axis]
        lower = lax.rem(index[axis] + size - 1, size)
        upper = lax.rem(index[axis] + 1, size)
        copies = []
        for side, peer in ((0, lower), (1, upper)):
            copy = pltpu.make_async_remote_copy(
                src_ref=send_buf.at[phase, side],
                dst_ref=recv_buf.at[phase, 1 - side],
                send_sem=halo_send.at[phase, side],
                recv_sem=halo_recv.at[phase, 1 - side],
                device_id={AXES[axis]: peer},
                device_id_type=MESH,
            )
            copy.start()
            copies.append(copy)
        pending.extend(copies)
        return copies

    def end_halo(phase, copies):
        for copy in copies:
            copy.wait_recv()
        before = recv_buf[phase, 0, 0:SIDE, :]
        after = recv_buf[phase, 1, 0:SIDE, :]
        top = jnp.where(left, before, pltpu.roll(after, SIDE, 1))
        bottom = jnp.where(left, pltpu.roll(before, SIDE, 1), after)
        field_q = jnp.where(left8, recv_buf[phase, 0, SIDE:MSG, :], recv_buf[phase, 1, SIDE:MSG, :])
        return jnp.concatenate([top, bottom], axis=0), field_q

    def set_block(step, start, width, field_x, field_q):
        cols = slice(start, start + width)
        tab_x[step, :, cols] = field_x
        tab_q[step, :, cols] = field_q
        left, right = slice(2 * start, 2 * start + width), slice(2 * start + width, 2 * start + 2 * width)
        high, low = split(field_x)
        tab_s[0:LAT, left] = high
        tab_s[0:LAT, right] = low
        tab_w[step, 0:LAT, cols] = high
        tab_w[step, LAT:, cols] = low
        tab_s[LAT:, left], tab_s[LAT:, right] = split_place(field_q)

    def project_block(step, start, width):
        cols = slice(2 * start, 2 * start + 2 * width)
        high, low = split(exact(w_t[0], tab_x[step, :, start : start + width]))
        tab_a[0:LAT, cols] = jnp.concatenate([high, low], axis=1)
        tab_a[LAT:, cols] = tab_s[LAT:, cols]

    def select(axis, start, width):
        return dot(tab_s[:, 2 * start : 2 * (start + width)], twice(sels[axis][start : start + width, :]))

    def send_rows(phase, axis, product):
        field_x, field_q = join_rows(product)
        low = jnp.where(index[axis] == 0, float(sizes[axis]), 0.0)
        high = jnp.where(index[axis] == sizes[axis] - 1, -float(sizes[axis]), 0.0)
        offset = jnp.where(row8 == axis, jnp.where(left8, low, high), 0.0)
        return start_halo(phase, axis, field_x, field_q + offset)

    def gather_block(start, width, extra=None):
        def body(n, carry):
            picker = twice(onehot[n, start : start + width, :])
            value, place = join_rows(dot(tab_a[:, 2 * start : 2 * (start + width)], picker))
            if extra is None:
                gath[n, 0:LAT, :] += value
                gath[n, LAT:, :] += place
            else:
                gath[n, 0:LAT, :] = value + extra[...]
                gath[n, LAT:, :] = place
            return carry

        lax.fori_loop(0, NBR, body, 0, unroll=UNROLL)

    def forward(step, phase, prologue):
        copies = send_rows(phase, 0, select(0, 0, OWN))
        prologue()
        project_block(step, 0, OWN)
        d_recv[...] = exact(w_t[1], tab_x[step, :, 0:OWN])
        early_y = select(1, 0, OWN)
        early_z = select(2, 0, OWN)
        gather_block(0, OWN, d_recv)
        start = OWN
        set_block(step, start, GHOST, *end_halo(phase, copies))
        copies = send_rows(phase + 1, 1, early_y + select(1, start, GHOST))
        early_z = early_z + select(2, start, GHOST)
        project_block(step, start, GHOST)
        gather_block(start, GHOST)
        start = start + GHOST
        set_block(step, start, GHOST, *end_halo(phase + 1, copies))
        copies = send_rows(phase + 2, 2, early_z + select(2, start, GHOST))
        project_block(step, start, GHOST)
        gather_block(start, GHOST)
        start = start + GHOST
        set_block(step, start, GHOST, *end_halo(phase + 2, copies))
        project_block(step, start, GHOST)
        own_q = tab_q[step, :, 0:OWN]
        counts = count_ref[...]
        summed[step] = jnp.zeros((LAT, OWN), F32)

        def body(n, carry):
            picker = twice(onehot[n, start : start + GHOST, :])
            value, place = join_rows(dot(tab_a[:, 2 * start : 2 * (start + GHOST)], picker))
            rel = gath[n, LAT:, :] + place - own_q
            dist = jnp.sum(rel * rel, axis=0, keepdims=True)
            geo = jnp.where(row8_own == 3, dist, rel)
            geos[step, n] = geo
            coarse = geo.astype(BF16).astype(F32)
            fine = geo - coarse
            rows = jnp.concatenate([coarse, fine, coarse, jnp.zeros_like(fine)], axis=0).astype(BF16)
            edge_rows[step, 2 * LAT :, edges_of(n)] = rows[0:16]
            pre = gath[n, 0:LAT, :] + value + dot(w_geo_k[...], rows)
            gate = 0.5 * jnp.tanh(0.5 * pre) + 0.5
            keep = (counts > n).astype(F32)
            gate_keep = gate * keep
            summed[step] += pre * gate_keep
            slope[step, n] = gate_keep * (1.0 + pre * (1.0 - gate))
            return carry

        lax.fori_loop(0, NBR, body, 0, unroll=UNROLL)
        new_x = tab_x[step, :, 0:OWN] + live * exact(w_t[2], summed[step])
        fresh[step] = new_x
        return new_x

    def scatter(start, width):
        def body(n, carry):
            return carry + dot_nt(dpre[:, edges_of(n)], onehot[n, start : start + width, :])

        product = lax.fori_loop(0, NBR, body, jnp.zeros((2 * LAT + 16, width), F32), unroll=UNROLL)
        return product[0:LAT] + product[LAT : 2 * LAT], product[256:264] + product[264:272]

    def gather_latents(step):
        def body(n, carry):
            edge_rows[step, 0 : 2 * LAT, edges_of(n)] = dot(tab_w[step], onehot[n]).astype(BF16)
            return carry

        lax.fori_loop(0, NBR, body, 0, unroll=UNROLL)

    def backward(step, phase, cot_v, cot_p, first, tail):
        move = STRIDE * live * cot_p
        full = cot_v
        for k in range(3):
            full = full + w_t[3, :, k : k + 1] * move[k : k + 1, :]
        d_agg = live * full
        d_sum = exact(w_msg_ref[...], d_agg)
        d_recv[...] = jnp.zeros((LAT, OWN), F32)
        d_place[...] = jnp.zeros((8, OWN), F32)

        def body(n, carry):
            value = d_sum * slope[step, n]
            geo = geos[step, n]
            high, low = split(value)
            cols = edges_of(n)
            dpre[0:LAT, cols] = high
            dpre[LAT : 2 * LAT, cols] = low
            d_recv[...] += value
            back = dot(w_geo_s[...], jnp.concatenate([high, low], axis=0))
            back = back[0:8] + back[8:16]
            d_rel = jnp.where(row8_own < 3, back + 2.0 * geo * back[3:4], 0.0)
            d_place[...] -= d_rel
            coarse = d_rel.astype(BF16).astype(F32)
            dpre[2 * LAT :, cols] = jnp.concatenate([coarse, d_rel - coarse], axis=0).astype(BF16)
            return carry

        lax.fori_loop(0, NBR, body, 0, unroll=UNROLL)

        def spread(start, width):
            d_send, d_q = scatter(start, width)
            return exact(w_send_ref[...], d_send), d_q

        def spread_block(start, width):
            cot_x[:, start : start + width], cot_q[:, start : start + width] = spread(start, width)

        def weights(d_weight, d_geo):
            pieces = (
                (0, LAT, d_weight),
                (LAT, LAT, exact_nt(tab_x[step, :, 0:OWN], d_recv[...])),
                (2 * LAT, LAT, exact_nt(summed[step], d_agg)),
                (3 * LAT, 8, d_geo),
                (3 * LAT + 8, 8, exact_nt(move, fresh[step])),
            )
            for base, rows, piece in pieces:
                if first:
                    grads[base : base + rows, :] = piece
                else:
                    grads[base : base + rows, :] += piece

        def by_edges():
            edge_sum[...] = jnp.zeros((2 * LAT + 16, 2 * LAT), F32)

            def body(n, carry):
                edge_sum[...] += dot_nt(edge_rows[step, :, edges_of(n)], dpre[0 : 2 * LAT, edges_of(n)])
                return carry

            lax.fori_loop(0, NBR, body, 0, unroll=UNROLL)
            product = edge_sum[...]
            geo = product[256:264, 0:LAT] + product[256:264, LAT:] + product[264:272, 0:LAT]
            return product[0:LAT, 0:LAT] + product[0:LAT, LAT:] + product[LAT : 2 * LAT, 0:LAT], geo

        if not first:
            weights(*by_edges())
            tail(0)
        copies = start_halo(phase, 2, *spread(OWN + 2 * GHOST, GHOST))
        tail(1)
        spread_block(OWN + GHOST, GHOST)
        if first:
            gather_latents(1)

        def arrived(number, axis, copies):
            field_x, field_q = end_halo(number, copies)
            high, low = split(field_x)
            left, right = split_place(field_q)
            rows = jnp.concatenate(
                [jnp.concatenate([high, low], axis=1), jnp.concatenate([left, right], axis=1)], axis=0
            )

            def add(start, width):
                extra, extra_q = join_rows(dot(rows, twice(backs[axis][:, start : start + width])))
                cot_x[:, start : start + width] += extra
                cot_q[:, start : start + width] += extra_q

            return add

        add = arrived(phase, 2, copies)
        start = OWN + GHOST
        add(start, GHOST)
        copies = start_halo(phase + 1, 1, cot_x[:, start : start + GHOST], cot_q[:, start : start + GHOST])
        tail(2)
        spread_block(OWN, GHOST)
        spread_block(0, OWN)
        cot_x[:, 0:OWN] += full + exact(w_recv_ref[...], d_recv[...])
        cot_q[:, 0:OWN] += cot_p + d_place[...]
        add(OWN, GHOST)
        add(0, OWN)
        add = arrived(phase + 1, 1, copies)
        start = OWN
        add(start, GHOST)
        copies = start_halo(phase + 2, 0, cot_x[:, start : start + GHOST], cot_q[:, start : start + GHOST])
        tail(3)
        add(0, OWN)
        if first:
            weights(*by_edges())
            gather_latents(0)
        add = arrived(phase + 2, 0, copies)
        add(0, OWN)
        return cot_x[:, 0:OWN], cot_q[:, 0:OWN]

    pad[...] = jnp.zeros((8, OWN), F32)
    pad[0:3, :] = position_ref[...]
    set_block(0, 0, OWN, jnp.transpose(latent_ref[...]), pad[...])
    selector(0)
    pl.semaphore_wait(barrier, partners)

    def prologue():
        for axis in range(3):
            backs[axis][...] = jnp.transpose(selector(axis)).astype(BF16)
        w_t[0] = jnp.transpose(w_send_ref[...])
        w_t[1] = jnp.transpose(w_recv_ref[...])
        w_t[2] = jnp.transpose(w_msg_ref[...])
        w_t[3] = jnp.zeros((LAT, LAT), F32)
        w_t[3, 0:3, :] = w_dec_ref[...]
        w_t[3] = jnp.transpose(w_t[3])
        w_t[4] = jnp.zeros((LAT, LAT), F32)
        w_t[4, 0:4, :] = w_geo_ref[...]
        w_geo = w_t[4, 0:8, :]
        coarse = w_geo.astype(BF16).astype(F32)
        fine = w_geo - coarse
        main = jnp.concatenate([coarse, fine], axis=0)
        side = jnp.concatenate([coarse, jnp.zeros_like(fine)], axis=0)
        w_geo_s[...] = jnp.concatenate([main, side], axis=1).astype(BF16)
        w_t[4, 0:8, :] = coarse
        w_t[4, 8:16, :] = coarse
        w_t[4, 16:24, :] = fine
        w_geo_k[...] = jnp.transpose(w_t[4])[:, 0:32].astype(BF16)
        grads[...] = jnp.zeros((GRAD_ROWS, LAT), F32)

        flat = senders_ref[...]
        spread = jnp.broadcast_to(flat[:, None, :], (OWN // 8, 8, LAT)).reshape(OWN, LAT)
        lanes = lax.broadcasted_iota(jnp.int32, (OWN, LAT), 1)
        sublanes = lax.broadcasted_iota(jnp.int32, (OWN, LAT), 0)
        mine = lanes // NBR == sublanes % 8
        rest = spread % 8
        slot = lax.broadcasted_iota(jnp.int32, (NBR, LAT), 1) % NBR == lax.broadcasted_iota(jnp.int32, (NBR, LAT), 0)
        slot = slot.astype(F32).astype(BF16)
        coarse = jnp.where(mine, spread - rest, 0).astype(F32).astype(BF16)
        fine = jnp.where(mine, rest, 0).astype(F32).astype(BF16)
        slots[...] = (dot_nt(slot, coarse) + dot_nt(slot, fine)).astype(jnp.int32)

        def body(n, carry):
            ids = lax.broadcasted_iota(jnp.int32, (ROWS, OWN), 0)
            onehot[n] = (ids == slots[pl.ds(n, 1), :]).astype(F32).astype(BF16)
            return carry

        lax.fori_loop(0, NBR, body, 0)

    new_x = forward(0, 0, prologue)
    w_dec = jnp.concatenate([w_dec_ref[...], jnp.zeros((5, LAT), F32)], axis=0)
    new_q = tab_q[0, :, 0:OWN] + STRIDE * live * exact(w_dec, new_x)
    set_block(1, 0, OWN, new_x, new_q)
    forward(1, 3, lambda: None)

    pad[0:3, :] = cot_position_ref[...]
    cot_v, cot_p = backward(1, 6, jnp.transpose(cot_latent_ref[...]), pad[...], True, lambda number: None)

    half = GRAD_ROWS // CORES
    piece = half // plane
    numbers = iter(range(2 + 2 * (plane - 1) + (ring - 1)))

    def push(source, target, peer):
        number = next(numbers)
        copy = pltpu.make_async_remote_copy(
            src_ref=source,
            dst_ref=target,
            send_sem=sum_send.at[number],
            recv_sem=sum_recv.at[number],
            device_id=peer,
            device_id_type=MESH,
        )
        copy.start()
        pending.append(copy)
        return copy

    def rows_of(base, count):
        return pl.ds(pl.multiple_of(base, 8), count)

    own_half = rows_of(core * half, half)
    own_piece = rows_of(core * half + at_plane * piece, piece)
    flying = []

    def arrive():
        for copy in flying:
            copy.wait_recv()
        flying.clear()

    def tail(number):
        if number == 0:
            flying.append(push(grads.at[rows_of((1 - core) * half, half), :], got_core, other_core))
        elif number == 1:
            arrive()
            part_half[...] = grads[own_half, :] + got_core[...]
            for k in range(1, plane):
                place, peer = plane_peer(k)
                flying.append(push(part_half.at[rows_of(place * piece, piece), :], got_plane.at[k - 1], peer))
        elif number == 2:
            arrive()
            value = part_half[rows_of(at_plane * piece, piece), :]
            for k in range(plane - 1):
                value = value + got_plane[k]
            part_ring[at_ring] = value
            for k in range(1, ring):
                flying.append(push(part_ring.at[at_ring], part_ring.at[at_ring], ring_peer(k)[1]))
        else:
            arrive()
            value = part_ring[0]
            for k in range(1, ring):
                value = value + part_ring[k]
            total[own_piece, :] = value * scale
            for k in range(1, plane):
                flying.append(push(total.at[own_piece, :], total.at[own_piece, :], plane_peer(k)[1]))

    cot_v, cot_p = backward(0, 9, cot_v, cot_p, False, tail)
    arrive()
    flying.append(push(total.at[own_half, :], total.at[own_half, :], other_core))
    out_latent_ref[...] = jnp.transpose(cot_v)
    out_position_ref[...] = cot_p[0:3]
    arrive()
    for copy in pending:
        copy.wait_send()


def hand_out(grad_x, grad_q, total, out_x, out_q, out_send, out_recv, out_geo, out_msg, out_dec, sems):
    pairs = (
        (grad_x, out_x),
        (grad_q, out_q),
        (total.at[0:LAT, :], out_send),
        (total.at[LAT : 2 * LAT, :], out_recv),
        (total.at[3 * LAT : 3 * LAT + 4, :], out_geo),
        (total.at[2 * LAT : 3 * LAT, :], out_msg),
        (total.at[3 * LAT + 8 : 3 * LAT + 11, :], out_dec),
    )
    copies = [pltpu.make_async_copy(source, target, sems.at[n]) for n, (source, target) in enumerate(pairs)]
    for copy in copies:
        copy.start()
    for copy in copies:
        copy.wait()


def per_device(sizes, scale, *args):
    (
        latent,
        position,
        particle_count,
        nbr_count,
        senders,
        ghost_x,
        ghost_y,
        ghost_z,
        w_send,
        w_recv,
        w_geo,
        w_msg,
        w_dec,
        cot_latent,
        cot_position,
    ) = args
    given = (
        latent,
        position,
        particle_count,
        nbr_count.reshape(1, OWN),
        senders.reshape(OWN * NBR // LAT, LAT),
        ghost_x,
        ghost_y,
        ghost_z,
        w_send,
        w_recv,
        w_geo,
        w_msg,
        w_dec,
        cot_latent,
        cot_position,
    )
    plane = sizes[0] // CORES * (sizes[1] // LOWS)
    ring = sizes[2] * LOWS
    half = GRAD_ROWS // CORES
    sums = 2 + 2 * (plane - 1) + (ring - 1)
    vmem = pl.BlockSpec(memory_space=pltpu.VMEM)
    anywhere = pl.BlockSpec(memory_space=pl.ANY)
    held = [(pltpu.SMEM if array.size == 1 else pltpu.VMEM)(array.shape, array.dtype) for array in given]
    grad_x, grad_q, total = pl.pallas_call(
        functools.partial(kernel, sizes, scale),
        out_shape=(
            jax.ShapeDtypeStruct((OWN, LAT), F32),
            jax.ShapeDtypeStruct((3, OWN), F32),
            jax.ShapeDtypeStruct((GRAD_ROWS, LAT), F32),
        ),
        in_specs=[pl.BlockSpec(memory_space=pltpu.HBM)] * INPUTS,
        out_specs=(vmem,) * 3,
        scratch_shapes=[
            *held,
            pltpu.SemaphoreType.DMA((INPUTS,)),
            pltpu.VMEM((NBR, ROWS, OWN), BF16),
            pltpu.VMEM((OWN, GHOST), BF16),
            pltpu.VMEM((OWN + GHOST, GHOST), BF16),
            pltpu.VMEM((OWN + 2 * GHOST, GHOST), BF16),
            pltpu.VMEM((GHOST, OWN), BF16),
            pltpu.VMEM((GHOST, OWN + GHOST), BF16),
            pltpu.VMEM((GHOST, OWN + 2 * GHOST), BF16),
            pltpu.VMEM((2, 2 * LAT + 16, NBR * OWN), BF16),
            pltpu.VMEM((2 * LAT + 16, 2 * LAT), F32),
            pltpu.VMEM((2, LAT, ROWS), F32),
            pltpu.VMEM((2, 8, ROWS), F32),
            pltpu.VMEM((LAT + 16, 2 * ROWS), BF16),
            pltpu.VMEM((2, 2 * LAT, ROWS), BF16),
            pltpu.VMEM((LAT + 16, 2 * ROWS), BF16),
            pltpu.VMEM((NBR, LAT + 8, OWN), F32),
            pltpu.VMEM((2, NBR, LAT, OWN), F32),
            pltpu.VMEM((2, NBR, 8, OWN), F32),
            pltpu.VMEM((2, LAT, OWN), F32),
            pltpu.VMEM((2, LAT, OWN), F32),
            pltpu.VMEM((2 * LAT + 16, NBR * OWN), BF16),
            pltpu.VMEM((LAT, OWN), F32),
            pltpu.VMEM((8, OWN), F32),
            pltpu.VMEM((LAT, ROWS), F32),
            pltpu.VMEM((8, ROWS), F32),
            pltpu.VMEM((8, OWN), F32),
            pltpu.VMEM((5, LAT, LAT), F32),
            pltpu.VMEM((LAT, 32), BF16),
            pltpu.VMEM((16, 2 * LAT), BF16),
            pltpu.VMEM((GRAD_ROWS, LAT), F32),
            pltpu.VMEM((half, LAT), F32),
            pltpu.VMEM((ring, half // plane, LAT), F32),
            pltpu.VMEM((half, LAT), F32),
            pltpu.VMEM((plane - 1, half // plane, LAT), F32),
            pltpu.VMEM((12, 2, MSG, GHOST), F32),
            pltpu.VMEM((12, 2, MSG, GHOST), F32),
            pltpu.SemaphoreType.DMA((12, 2)),
            pltpu.SemaphoreType.DMA((12, 2)),
            pltpu.SemaphoreType.DMA((sums,)),
            pltpu.SemaphoreType.DMA((sums,)),
            pltpu.VMEM((NBR, OWN), jnp.int32),
        ],
        compiler_params=pltpu.CompilerParams(
            collective_id=0, has_side_effects=True, vmem_limit_bytes=64 * 1024 * 1024
        ),
        name="evolver_backward",
    )(*given)
    return pl.pallas_call(
        hand_out,
        out_shape=(
            jax.ShapeDtypeStruct((OWN, LAT), F32),
            jax.ShapeDtypeStruct((3, OWN), F32),
            jax.ShapeDtypeStruct((LAT, LAT), F32),
            jax.ShapeDtypeStruct((LAT, LAT), F32),
            jax.ShapeDtypeStruct((4, LAT), F32),
            jax.ShapeDtypeStruct((LAT, LAT), F32),
            jax.ShapeDtypeStruct((3, LAT), F32),
        ),
        in_specs=[vmem] * 3,
        out_specs=(anywhere,) * 7,
        scratch_shapes=[pltpu.SemaphoreType.DMA((7,))],
        name="hand_out",
    )(grad_x, grad_q, total)


def solution(mesh):
    sizes = tuple(mesh.shape[axis] for axis in AXES)
    scale = 1.0 / math.sqrt(sizes[0] * sizes[1] * sizes[2] * OWN)
    whole = P(AXES)
    rows = P(AXES, None)
    columns = P(None, AXES)
    placed = (rows, columns, whole, whole, whole, rows, rows, rows) + (P(),) * 5 + (rows, columns)
    return jax.shard_map(
        functools.partial(per_device, sizes, scale),
        mesh=mesh,
        in_specs=placed,
        out_specs=(rows, columns) + (P(),) * 5,
        check_vma=False,
    )
```

```python
import functools
import math

import jax
import jax.numpy as jnp
from jax import lax
from jax.experimental import pallas as pl
from jax.experimental.pallas import tpu as pltpu
from jax.sharding import PartitionSpec as P

MESH = pl.DeviceIdType.MESH
AXES = ("gx", "gy", "gz")
F32 = jnp.float32
BF16 = jnp.bfloat16
STRIDE = 0.1
LAT = 128
OWN = 256
NBR = 16
SIDE = 64
GHOST = 2 * SIDE
ROWS = OWN + 3 * GHOST
GRAD_ROWS = 512
MSG = SIDE + 8
UNROLL = 8
INPUTS = 15
CORES = 2
LOWS = 2


def dot(left, right):
    return lax.dot_general(left, right, (((1,), (0,)), ((), ())), preferred_element_type=F32)


def dot_nt(left, right):
    return lax.dot_general(left, right, (((1,), (1,)), ((), ())), preferred_element_type=F32)


def split(value):
    high = value.astype(BF16)
    return high, (value - high.astype(F32)).astype(BF16)


def exact(left, right):
    left_high, left_low = split(left)
    right_high, right_low = split(right)
    return dot(
        jnp.concatenate([left_high, left_low, left_high], axis=1),
        jnp.concatenate([right_high, right_high, right_low], axis=0),
    )


def exact_nt(left, right):
    left_high, left_low = split(left)
    right_high, right_low = split(right)
    return dot_nt(
        jnp.concatenate([left_high, left_low, left_high], axis=1),
        jnp.concatenate([right_high, right_high, right_low], axis=1),
    )


def split_place(field_q):
    first = field_q.astype(BF16).astype(F32)
    rest = field_q - first
    second = rest.astype(BF16).astype(F32)
    third = rest - second
    left = jnp.concatenate([first, third], axis=0).astype(BF16)
    right = jnp.concatenate([second, jnp.zeros_like(third)], axis=0).astype(BF16)
    return left, right


def twice(picker):
    return jnp.concatenate([picker, picker], axis=0)


def join_rows(product):
    return product[0:LAT], product[LAT : LAT + 8] + product[LAT + 8 : LAT + 16]


def kernel(
    sizes,
    scale,
    *refs,
):
    given = refs[:INPUTS]
    out_latent_ref, out_position_ref, total = refs[INPUTS : INPUTS + 3]
    held = refs[INPUTS + 3 : 2 * INPUTS + 3]
    load_sem = refs[2 * INPUTS + 3]
    body(sizes, scale, given, held, load_sem, out_latent_ref, out_position_ref, total, *refs[2 * INPUTS + 4 :])


def body(
    sizes,
    scale,
    given,
    held,
    load_sem,
    out_latent_ref,
    out_position_ref,
    total,
    onehot,
    sel_x,
    sel_y,
    sel_z,
    back_x,
    back_y,
    back_z,
    edge_rows,
    edge_sum,
    moved,
    fulls,
    d_sum,
    d_back,
    tab_x,
    tab_q,
    tab_s,
    tab_w,
    tab_a,
    gath,
    slope,
    geos,
    summed,
    fresh,
    dpre,
    d_recv,
    d_place,
    cot_x,
    cot_q,
    pad,
    w_t,
    w_geo_k,
    w_geo_s,
    grads,
    part_half,
    part_ring,
    got_core,
    got_plane,
    send_buf,
    recv_buf,
    halo_send,
    halo_recv,
    sum_send,
    sum_recv,
    slots,
):
    (
        latent_ref,
        position_ref,
        particles_ref,
        count_ref,
        senders_ref,
        ghost_x_ref,
        ghost_y_ref,
        ghost_z_ref,
        w_send_ref,
        w_recv_ref,
        w_geo_ref,
        w_msg_ref,
        w_dec_ref,
        cot_latent_ref,
        cot_position_ref,
    ) = held
    ghost_refs = (ghost_x_ref, ghost_y_ref, ghost_z_ref)
    loads = [
        pltpu.make_async_copy(source, target, load_sem.at[number])
        for number, (source, target) in enumerate(zip(given, held))
    ]
    index = tuple(lax.axis_index(axis) for axis in AXES)
    sels = (sel_x, sel_y, sel_z)
    backs = (back_x, back_y, back_z)

    barrier = pltpu.get_barrier_semaphore()
    core, y = lax.rem(index[0], CORES), lax.div(index[0], CORES)
    lows, xs = LOWS, sizes[1] // LOWS
    x, low = lax.rem(index[1], xs), lax.div(index[1], xs)
    plane, ring = sizes[0] // CORES * xs, sizes[2] * lows
    at_plane, at_ring = y * xs + x, index[2] * lows + low

    def plane_peer(k):
        place = lax.rem(at_plane + k, plane)
        return place, {"gx": lax.div(place, xs) * CORES + core, "gy": low * xs + lax.rem(place, xs)}

    def ring_peer(k):
        place = lax.rem(at_ring + k, ring)
        return place, {"gy": lax.rem(place, lows) * xs + x, "gz": lax.div(place, lows)}

    other_core = {"gx": y * CORES + 1 - core}
    greeted = [plane_peer(k)[1] for k in range(1, plane)] + [ring_peer(k)[1] for k in range(1, ring)]
    for axis in (0, 1):
        for step in (1, sizes[axis] - 1):
            greeted.append({AXES[axis]: lax.rem(index[axis] + step, sizes[axis])})
    for peer in greeted:
        pl.semaphore_signal(barrier, inc=1, device_id=peer, device_id_type=MESH)
    partners = len(greeted)
    early = (0, 1, 2, 5, 6, 7)
    order = early + tuple(number for number in range(INPUTS) if number not in early)
    for number in order:
        loads[number].start()

    lane = lax.broadcasted_iota(jnp.int32, (SIDE, GHOST), 1)
    left = lane < SIDE
    left8 = left[0:8]
    row8 = lax.broadcasted_iota(jnp.int32, (8, GHOST), 0)
    row8_own = lax.broadcasted_iota(jnp.int32, (8, OWN), 0)
    for number in early:
        loads[number].wait()
    live = (lax.broadcasted_iota(jnp.int32, (1, OWN), 1) < particles_ref[0]).astype(F32)

    def selector(axis):
        rows = OWN + axis * GHOST
        lists = ghost_refs[axis][...]
        chosen = jnp.concatenate([lists[0:1], lists[1:2]], axis=1)
        ids = lax.broadcasted_iota(jnp.int32, (rows, GHOST), 0)
        picked = (ids == chosen).astype(F32)
        sels[axis][...] = picked.astype(BF16)
        return picked

    def edges_of(n):
        return pl.ds(pl.multiple_of(n * OWN, OWN), OWN)

    pending = []

    def start_halo(phase, axis, field_x, field_q):
        turned = pltpu.roll(field_x, SIDE, 1)
        turned_q = pltpu.roll(field_q, SIDE, 1)
        send_buf[phase, 0, 0:SIDE, :] = jnp.where(left, field_x[0:SIDE], turned[SIDE:])
        send_buf[phase, 0, SIDE:MSG, :] = turned_q
        send_buf[phase, 1, 0:SIDE, :] = jnp.where(left, turned[0:SIDE], field_x[SIDE:])
        send_buf[phase, 1, SIDE:MSG, :] = turned_q
        size = sizes[axis]
        lower = lax.rem(index[axis] + size - 1, size)
        upper = lax.rem(index[axis] + 1, size)
        copies = []
        if phase == 0:
            pl.semaphore_wait(barrier, partners)
        for side, peer in ((0, lower), (1, upper)):
            copy = pltpu.make_async_remote_copy(
                src_ref=send_buf.at[phase, side],
                dst_ref=recv_buf.at[phase, 1 - side],
                send_sem=halo_send.at[phase, side],
                recv_sem=halo_recv.at[phase, 1 - side],
                device_id={AXES[axis]: peer},
                device_id_type=MESH,
            )
            copy.start()
            copies.append(copy)
        pending.extend(copies)
        return copies

    def end_halo(phase, copies):
        for copy in copies:
            copy.wait_recv()
        before = recv_buf[phase, 0, 0:SIDE, :]
        after = recv_buf[phase, 1, 0:SIDE, :]
        top = jnp.where(left, before, pltpu.roll(after, SIDE, 1))
        bottom = jnp.where(left, pltpu.roll(before, SIDE, 1), after)
        field_q = jnp.where(left8, recv_buf[phase, 0, SIDE:MSG, :], recv_buf[phase, 1, SIDE:MSG, :])
        return jnp.concatenate([top, bottom], axis=0), field_q

    def set_block(step, start, width, field_x, field_q):
        cols = slice(start, start + width)
        tab_x[step, :, cols] = field_x
        tab_q[step, :, cols] = field_q
        left, right = slice(2 * start, 2 * start + width), slice(2 * start + width, 2 * start + 2 * width)
        high, low = split(field_x)
        tab_s[0:LAT, left] = high
        tab_s[0:LAT, right] = low
        tab_w[step, 0:LAT, cols] = high
        tab_w[step, LAT:, cols] = low
        tab_s[LAT:, left], tab_s[LAT:, right] = split_place(field_q)

    def project_block(step, start, width):
        cols = slice(2 * start, 2 * start + 2 * width)
        high, low = split(exact(w_t[0], tab_x[step, :, start : start + width]))
        tab_a[0:LAT, cols] = jnp.concatenate([high, low], axis=1)
        tab_a[LAT:, cols] = tab_s[LAT:, cols]

    def select(axis, start, width):
        return dot(tab_s[:, 2 * start : 2 * (start + width)], twice(sels[axis][start : start + width, :]))

    def send_rows(phase, axis, product):
        field_x, field_q = join_rows(product)
        low = jnp.where(index[axis] == 0, float(sizes[axis]), 0.0)
        high = jnp.where(index[axis] == sizes[axis] - 1, -float(sizes[axis]), 0.0)
        offset = jnp.where(row8 == axis, jnp.where(left8, low, high), 0.0)
        return start_halo(phase, axis, field_x, field_q + offset)

    def gather_block(start, width, extra=None):
        def body(n, carry):
            picker = twice(onehot[n, start : start + width, :])
            value, place = join_rows(dot(tab_a[:, 2 * start : 2 * (start + width)], picker))
            if extra is None:
                gath[n, 0:LAT, :] += value
                gath[n, LAT:, :] += place
            else:
                gath[n, 0:LAT, :] = value + extra[...]
                gath[n, LAT:, :] = place
            return carry

        lax.fori_loop(0, NBR, body, 0, unroll=UNROLL)

    def prepare(cot_v, cot_p):
        move = STRIDE * live * cot_p
        full = cot_v
        for k in range(3):
            full = full + w_t[3, :, k : k + 1] * move[k : k + 1, :]
        d_agg = live * full
        moved[...] = move
        fulls[...] = full
        d_sum[...] = exact(w_msg_ref[...], d_agg)
        d_back[...] = jnp.zeros((LAT, OWN), F32)
        d_place[...] = jnp.zeros((8, OWN), F32)

    def push_back(n, slope_n, geo):
        value = d_sum[...] * slope_n
        high, low = split(value)
        cols = edges_of(n)
        dpre[0:LAT, cols] = high
        dpre[LAT : 2 * LAT, cols] = low
        d_back[...] += value
        back = dot(w_geo_s[...], jnp.concatenate([high, low], axis=0))
        back = back[0:8] + back[8:16]
        d_rel = jnp.where(row8_own < 3, back + 2.0 * geo * back[3:4], 0.0)
        d_place[...] -= d_rel
        coarse = d_rel.astype(BF16).astype(F32)
        dpre[2 * LAT :, cols] = jnp.concatenate([coarse, d_rel - coarse], axis=0).astype(BF16)

    def forward(step, phase, prologue, beside):
        copies = send_rows(phase, 0, select(0, 0, OWN))
        prologue()
        project_block(step, 0, OWN)
        d_recv[...] = exact(w_t[1], tab_x[step, :, 0:OWN])
        early_y = select(1, 0, OWN)
        early_z = select(2, 0, OWN)
        gather_block(0, OWN, d_recv)
        beside()
        start = OWN
        set_block(step, start, GHOST, *end_halo(phase, copies))
        copies = send_rows(phase + 1, 1, early_y + select(1, start, GHOST))
        early_z = early_z + select(2, start, GHOST)
        project_block(step, start, GHOST)
        gather_block(start, GHOST)
        start = start + GHOST
        set_block(step, start, GHOST, *end_halo(phase + 1, copies))
        copies = send_rows(phase + 2, 2, early_z + select(2, start, GHOST))
        project_block(step, start, GHOST)
        gather_block(start, GHOST)
        start = start + GHOST
        set_block(step, start, GHOST, *end_halo(phase + 2, copies))
        project_block(step, start, GHOST)
        own_q = tab_q[step, :, 0:OWN]
        counts = count_ref[...]
        summed[step] = jnp.zeros((LAT, OWN), F32)

        def body(n, carry):
            product = dot(tab_a[LAT:, 2 * start : 2 * (start + GHOST)], twice(onehot[n, start : start + GHOST, :]))
            rel = gath[n, LAT:, :] + (product[0:8] + product[8:16]) - own_q
            dist = jnp.sum(rel * rel, axis=0, keepdims=True)
            geo = jnp.where(row8_own == 3, dist, rel)
            geos[step, n] = geo
            coarse = geo.astype(BF16).astype(F32)
            edge_rows[step, 2 * LAT :, edges_of(n)] = jnp.concatenate([coarse, geo - coarse], axis=0).astype(BF16)
            return carry

        lax.fori_loop(0, NBR, body, 0, unroll=UNROLL)

        def body(n, carry):
            picker = twice(onehot[n, start : start + GHOST, :])
            value = dot(tab_a[0:LAT, 2 * start : 2 * (start + GHOST)], picker)
            rows = twice(edge_rows[step, 2 * LAT :, edges_of(n)])
            pre = gath[n, 0:LAT, :] + value + dot(w_geo_k[...], rows)
            gate = 0.5 * jnp.tanh(0.5 * pre) + 0.5
            keep = (counts > n).astype(F32)
            gate_keep = gate * keep
            summed[step] += pre * gate_keep
            slope[step, n] = gate_keep * (1.0 + pre * (1.0 - gate))
            return carry

        lax.fori_loop(0, NBR, body, 0, unroll=UNROLL)

    def update(step):
        new_x = tab_x[step, :, 0:OWN] + live * exact(w_t[2], summed[step])
        fresh[step] = new_x
        return new_x

    def scatter(start, width):
        def body(n, carry):
            return carry + dot_nt(dpre[:, edges_of(n)], onehot[n, start : start + width, :])

        product = lax.fori_loop(0, NBR, body, jnp.zeros((2 * LAT + 16, width), F32), unroll=UNROLL)
        return product[0:LAT] + product[LAT : 2 * LAT], product[256:264] + product[264:272]

    def gather_latents(step):
        def body(n, carry):
            edge_rows[step, 0 : 2 * LAT, edges_of(n)] = dot(tab_w[step], onehot[n]).astype(BF16)
            return carry

        lax.fori_loop(0, NBR, body, 0, unroll=UNROLL)

    def backward(step, phase, cot_v, cot_p, first, tail):
        if not first:
            prepare(cot_v, cot_p)

        def body(n, carry):
            push_back(n, slope[step, n], geos[step, n])
            return carry

        lax.fori_loop(0, NBR, body, 0, unroll=UNROLL)

        def spread(start, width):
            d_send, d_q = scatter(start, width)
            return exact(w_send_ref[...], d_send), d_q

        def spread_block(start, width):
            cot_x[:, start : start + width], cot_q[:, start : start + width] = spread(start, width)

        def weights(d_weight, d_geo):
            if first:
                update(step)
            pieces = (
                (0, LAT, d_weight),
                (LAT, LAT, exact_nt(tab_x[step, :, 0:OWN], d_back[...])),
                (2 * LAT, LAT, exact_nt(summed[step], live * fulls[...])),
                (3 * LAT, 8, d_geo),
                (3 * LAT + 8, 8, exact_nt(moved[...], fresh[step])),
            )
            for base, rows, piece in pieces:
                if first:
                    grads[base : base + rows, :] = piece
                else:
                    grads[base : base + rows, :] += piece

        def by_edges():
            edge_sum[...] = jnp.zeros((2 * LAT + 16, 2 * LAT), F32)

            def body(n, carry):
                edge_sum[...] += dot_nt(edge_rows[step, :, edges_of(n)], dpre[0 : 2 * LAT, edges_of(n)])
                return carry

            lax.fori_loop(0, NBR, body, 0, unroll=UNROLL)
            product = edge_sum[...]
            geo = product[256:264, 0:LAT] + product[256:264, LAT:] + product[264:272, 0:LAT]
            return product[0:LAT, 0:LAT] + product[0:LAT, LAT:] + product[LAT : 2 * LAT, 0:LAT], geo

        if not first:
            weights(*by_edges())
            tail(0)
        copies = start_halo(phase, 2, *spread(OWN + 2 * GHOST, GHOST))
        tail(1)
        spread_block(OWN + GHOST, GHOST)
        if first:
            gather_latents(1)

        def arrived(number, axis, copies):
            field_x, field_q = end_halo(number, copies)
            high, low = split(field_x)
            left, right = split_place(field_q)
            rows = jnp.concatenate(
                [jnp.concatenate([high, low], axis=1), jnp.concatenate([left, right], axis=1)], axis=0
            )

            def add(start, width):
                extra, extra_q = join_rows(dot(rows, twice(backs[axis][:, start : start + width])))
                cot_x[:, start : start + width] += extra
                cot_q[:, start : start + width] += extra_q

            return add

        add = arrived(phase, 2, copies)
        start = OWN + GHOST
        add(start, GHOST)
        copies = start_halo(phase + 1, 1, cot_x[:, start : start + GHOST], cot_q[:, start : start + GHOST])
        tail(2)
        spread_block(OWN, GHOST)
        spread_block(0, OWN)
        cot_x[:, 0:OWN] += fulls[...] + exact(w_recv_ref[...], d_back[...])
        cot_q[:, 0:OWN] += cot_p + d_place[...]
        add(OWN, GHOST)
        add(0, OWN)
        add = arrived(phase + 1, 1, copies)
        start = OWN
        add(start, GHOST)
        copies = start_halo(phase + 2, 0, cot_x[:, start : start + GHOST], cot_q[:, start : start + GHOST])
        tail(3)
        add(0, OWN)
        if first:
            weights(*by_edges())
            gather_latents(0)
        add = arrived(phase + 2, 0, copies)
        add(0, OWN)
        return cot_x[:, 0:OWN], cot_q[:, 0:OWN]

    pad[...] = jnp.zeros((8, OWN), F32)
    pad[0:3, :] = position_ref[...]
    set_block(0, 0, OWN, jnp.transpose(latent_ref[...]), pad[...])
    selector(0)

    def prologue():
        for number in order[len(early) :]:
            loads[number].wait()
        for axis in range(3):
            backs[axis][...] = jnp.transpose(selector(axis)).astype(BF16)
        w_t[0] = jnp.transpose(w_send_ref[...])
        w_t[1] = jnp.transpose(w_recv_ref[...])
        w_t[2] = jnp.transpose(w_msg_ref[...])
        w_t[3] = jnp.zeros((LAT, LAT), F32)
        w_t[3, 0:3, :] = w_dec_ref[...]
        w_t[3] = jnp.transpose(w_t[3])
        w_t[4] = jnp.zeros((LAT, LAT), F32)
        w_t[4, 0:4, :] = w_geo_ref[...]
        w_geo = w_t[4, 0:8, :]
        coarse = w_geo.astype(BF16).astype(F32)
        fine = w_geo - coarse
        main = jnp.concatenate([coarse, fine], axis=0)
        side = jnp.concatenate([coarse, jnp.zeros_like(fine)], axis=0)
        w_geo_s[...] = jnp.concatenate([main, side], axis=1).astype(BF16)
        w_t[4, 0:8, :] = coarse
        w_t[4, 8:16, :] = coarse
        w_t[4, 16:24, :] = fine
        w_geo_k[...] = jnp.transpose(w_t[4])[:, 0:32].astype(BF16)
        grads[...] = jnp.zeros((GRAD_ROWS, LAT), F32)

        flat = senders_ref[...]
        spread = jnp.broadcast_to(flat[:, None, :], (OWN // 8, 8, LAT)).reshape(OWN, LAT)
        lanes = lax.broadcasted_iota(jnp.int32, (OWN, LAT), 1)
        sublanes = lax.broadcasted_iota(jnp.int32, (OWN, LAT), 0)
        mine = lanes // NBR == sublanes % 8
        rest = spread % 8
        slot = lax.broadcasted_iota(jnp.int32, (NBR, LAT), 1) % NBR == lax.broadcasted_iota(jnp.int32, (NBR, LAT), 0)
        slot = slot.astype(F32).astype(BF16)
        coarse = jnp.where(mine, spread - rest, 0).astype(F32).astype(BF16)
        fine = jnp.where(mine, rest, 0).astype(F32).astype(BF16)
        slots[...] = (dot_nt(slot, coarse) + dot_nt(slot, fine)).astype(jnp.int32)

        def body(n, carry):
            ids = lax.broadcasted_iota(jnp.int32, (ROWS, OWN), 0)
            onehot[n] = (ids == slots[pl.ds(n, 1), :]).astype(F32).astype(BF16)
            return carry

        lax.fori_loop(0, NBR, body, 0)

    forward(0, 0, prologue, lambda: None)
    new_x = update(0)
    w_dec = jnp.concatenate([w_dec_ref[...], jnp.zeros((5, LAT), F32)], axis=0)
    new_q = tab_q[0, :, 0:OWN] + STRIDE * live * exact(w_dec, new_x)
    set_block(1, 0, OWN, new_x, new_q)

    def beside():
        pad[0:3, :] = cot_position_ref[...]
        prepare(jnp.transpose(cot_latent_ref[...]), pad[...])

    forward(1, 3, lambda: None, beside)
    cot_v, cot_p = backward(1, 6, None, pad[...], True, lambda number: None)

    half = GRAD_ROWS // CORES
    piece = half // plane
    numbers = iter(range(2 + 2 * (plane - 1) + (ring - 1)))

    def push(source, target, peer):
        number = next(numbers)
        copy = pltpu.make_async_remote_copy(
            src_ref=source,
            dst_ref=target,
            send_sem=sum_send.at[number],
            recv_sem=sum_recv.at[number],
            device_id=peer,
            device_id_type=MESH,
        )
        copy.start()
        pending.append(copy)
        return copy

    def rows_of(base, count):
        return pl.ds(pl.multiple_of(base, 8), count)

    own_half = rows_of(core * half, half)
    own_piece = rows_of(core * half + at_plane * piece, piece)
    flying = []

    def arrive():
        for copy in flying:
            copy.wait_recv()
        flying.clear()

    def tail(number):
        if number == 0:
            flying.append(push(grads.at[rows_of((1 - core) * half, half), :], got_core, other_core))
        elif number == 1:
            arrive()
            part_half[...] = grads[own_half, :] + got_core[...]
            for k in range(1, plane):
                place, peer = plane_peer(k)
                flying.append(push(part_half.at[rows_of(place * piece, piece), :], got_plane.at[k - 1], peer))
        elif number == 2:
            arrive()
            value = part_half[rows_of(at_plane * piece, piece), :]
            for k in range(plane - 1):
                value = value + got_plane[k]
            part_ring[at_ring] = value
            for k in range(1, ring):
                flying.append(push(part_ring.at[at_ring], part_ring.at[at_ring], ring_peer(k)[1]))
        else:
            arrive()
            value = part_ring[0]
            for k in range(1, ring):
                value = value + part_ring[k]
            total[own_piece, :] = value * scale
            for k in range(1, plane):
                flying.append(push(total.at[own_piece, :], total.at[own_piece, :], plane_peer(k)[1]))

    cot_v, cot_p = backward(0, 9, cot_v, cot_p, False, tail)
    arrive()
    flying.append(push(total.at[own_half, :], total.at[own_half, :], other_core))
    out_latent_ref[...] = jnp.transpose(cot_v)
    out_position_ref[...] = cot_p[0:3]
    arrive()
    for copy in pending:
        copy.wait_send()


def hand_out(grad_x, grad_q, total, out_x, out_q, out_send, out_recv, out_geo, out_msg, out_dec, sems):
    pairs = (
        (grad_x, out_x),
        (grad_q, out_q),
        (total.at[0:LAT, :], out_send),
        (total.at[LAT : 2 * LAT, :], out_recv),
        (total.at[3 * LAT : 3 * LAT + 4, :], out_geo),
        (total.at[2 * LAT : 3 * LAT, :], out_msg),
        (total.at[3 * LAT + 8 : 3 * LAT + 11, :], out_dec),
    )
    copies = [pltpu.make_async_copy(source, target, sems.at[n]) for n, (source, target) in enumerate(pairs)]
    for copy in copies:
        copy.start()
    for copy in copies:
        copy.wait()


def per_device(sizes, scale, *args):
    (
        latent,
        position,
        particle_count,
        nbr_count,
        senders,
        ghost_x,
        ghost_y,
        ghost_z,
        w_send,
        w_recv,
        w_geo,
        w_msg,
        w_dec,
        cot_latent,
        cot_position,
    ) = args
    given = (
        latent,
        position,
        particle_count,
        nbr_count.reshape(1, OWN),
        senders.reshape(OWN * NBR // LAT, LAT),
        ghost_x,
        ghost_y,
        ghost_z,
        w_send,
        w_recv,
        w_geo,
        w_msg,
        w_dec,
        cot_latent,
        cot_position,
    )
    plane = sizes[0] // CORES * (sizes[1] // LOWS)
    ring = sizes[2] * LOWS
    half = GRAD_ROWS // CORES
    sums = 2 + 2 * (plane - 1) + (ring - 1)
    vmem = pl.BlockSpec(memory_space=pltpu.VMEM)
    anywhere = pl.BlockSpec(memory_space=pl.ANY)
    held = [(pltpu.SMEM if array.size == 1 else pltpu.VMEM)(array.shape, array.dtype) for array in given]
    grad_x, grad_q, total = pl.pallas_call(
        functools.partial(kernel, sizes, scale),
        out_shape=(
            jax.ShapeDtypeStruct((OWN, LAT), F32),
            jax.ShapeDtypeStruct((3, OWN), F32),
            jax.ShapeDtypeStruct((GRAD_ROWS, LAT), F32),
        ),
        in_specs=[pl.BlockSpec(memory_space=pltpu.HBM)] * INPUTS,
        out_specs=(vmem,) * 3,
        scratch_shapes=[
            *held,
            pltpu.SemaphoreType.DMA((INPUTS,)),
            pltpu.VMEM((NBR, ROWS, OWN), BF16),
            pltpu.VMEM((OWN, GHOST), BF16),
            pltpu.VMEM((OWN + GHOST, GHOST), BF16),
            pltpu.VMEM((OWN + 2 * GHOST, GHOST), BF16),
            pltpu.VMEM((GHOST, OWN), BF16),
            pltpu.VMEM((GHOST, OWN + GHOST), BF16),
            pltpu.VMEM((GHOST, OWN + 2 * GHOST), BF16),
            pltpu.VMEM((2, 2 * LAT + 16, NBR * OWN), BF16),
            pltpu.VMEM((2 * LAT + 16, 2 * LAT), F32),
            pltpu.VMEM((8, OWN), F32),
            pltpu.VMEM((LAT, OWN), F32),
            pltpu.VMEM((LAT, OWN), F32),
            pltpu.VMEM((LAT, OWN), F32),
            pltpu.VMEM((2, LAT, ROWS), F32),
            pltpu.VMEM((2, 8, ROWS), F32),
            pltpu.VMEM((LAT + 16, 2 * ROWS), BF16),
            pltpu.VMEM((2, 2 * LAT, ROWS), BF16),
            pltpu.VMEM((LAT + 16, 2 * ROWS), BF16),
            pltpu.VMEM((NBR, LAT + 8, OWN), F32),
            pltpu.VMEM((2, NBR, LAT, OWN), F32),
            pltpu.VMEM((2, NBR, 8, OWN), F32),
            pltpu.VMEM((2, LAT, OWN), F32),
            pltpu.VMEM((2, LAT, OWN), F32),
            pltpu.VMEM((2 * LAT + 16, NBR * OWN), BF16),
            pltpu.VMEM((LAT, OWN), F32),
            pltpu.VMEM((8, OWN), F32),
            pltpu.VMEM((LAT, ROWS), F32),
            pltpu.VMEM((8, ROWS), F32),
            pltpu.VMEM((8, OWN), F32),
            pltpu.VMEM((5, LAT, LAT), F32),
            pltpu.VMEM((LAT, 32), BF16),
            pltpu.VMEM((16, 2 * LAT), BF16),
            pltpu.VMEM((GRAD_ROWS, LAT), F32),
            pltpu.VMEM((half, LAT), F32),
            pltpu.VMEM((ring, half // plane, LAT), F32),
            pltpu.VMEM((half, LAT), F32),
            pltpu.VMEM((plane - 1, half // plane, LAT), F32),
            pltpu.VMEM((12, 2, MSG, GHOST), F32),
            pltpu.VMEM((12, 2, MSG, GHOST), F32),
            pltpu.SemaphoreType.DMA((12, 2)),
            pltpu.SemaphoreType.DMA((12, 2)),
            pltpu.SemaphoreType.DMA((sums,)),
            pltpu.SemaphoreType.DMA((sums,)),
            pltpu.VMEM((NBR, OWN), jnp.int32),
        ],
        compiler_params=pltpu.CompilerParams(
            collective_id=0, has_side_effects=True, vmem_limit_bytes=64 * 1024 * 1024
        ),
        name="evolver_backward",
    )(*given)
    return pl.pallas_call(
        hand_out,
        out_shape=(
            jax.ShapeDtypeStruct((OWN, LAT), F32),
            jax.ShapeDtypeStruct((3, OWN), F32),
            jax.ShapeDtypeStruct((LAT, LAT), F32),
            jax.ShapeDtypeStruct((LAT, LAT), F32),
            jax.ShapeDtypeStruct((4, LAT), F32),
            jax.ShapeDtypeStruct((LAT, LAT), F32),
            jax.ShapeDtypeStruct((3, LAT), F32),
        ),
        in_specs=[vmem] * 3,
        out_specs=(anywhere,) * 7,
        scratch_shapes=[pltpu.SemaphoreType.DMA((7,))],
        name="hand_out",
    )(grad_x, grad_q, total)


def solution(mesh):
    sizes = tuple(mesh.shape[axis] for axis in AXES)
    scale = 1.0 / math.sqrt(sizes[0] * sizes[1] * sizes[2] * OWN)
    whole = P(AXES)
    rows = P(AXES, None)
    columns = P(None, AXES)
    placed = (rows, columns, whole, whole, whole, rows, rows, rows) + (P(),) * 5 + (rows, columns)
    return jax.shard_map(
        functools.partial(per_device, sizes, scale),
        mesh=mesh,
        in_specs=placed,
        out_specs=(rows, columns) + (P(),) * 5,
        check_vma=False,
    )
```
